512 devices in a mesh: grp: 8 (over x, y_hi), slab: 64 (over z, y_lo, core).
Axes of the slice: x: 4, y: 4 (y_hi: 2, y_lo: 2; y = y_hi * 2 + y_lo), z: 16, core: 2. Of those that a mesh axis runs over, the one named last changes fastest.
Arguments:
- vectors: float32 [262144, 256], P(('grp', 'slab')), may hold values from -6 to 6
- diag_block: float32 [262144, 512], P(('grp', 'slab')), may hold values from -0.25 to 0.25
- slab_tiles: float32 [262144, 512], P(('grp', 'slab')), may hold values from -0.4375 to 0.4375
- slab_mask: int32 [2048, 4], P(('grp', 'slab')), may hold values from 0 to 1, as said below
- grp_tiles: float32 [262144, 512], P(('grp', 'slab')), may hold values from -0.4375 to 0.4375
- grp_mask: int32 [2048, 4], P(('grp', 'slab')), may hold values from 0 to 1, as said below
Outputs:
- filtered: float32 [262144, 256], P(('grp', 'slab'))
The draws below stay inside these ranges and needn't reach their ends.
Inputs may be any that keep to these rules, and one draw needn't show every extreme that they name: `slab_mask`: in every slab's 4 x 4 block of tiles toward its slab partner at least one tile is stored. `grp_mask`: in every slab's 4 x 4 block of tiles toward its group partner at least one tile is stored.
All inputs are finite; a program needn't handle non-finite values.
Results may differ from the reference program's by a relative error of at most 0.00005.
Values sent between devices are 32-bit elements; how exact they have to be, the bound alone decides.
No kernel may reach another device: no remote copies, remote signals or barrier semaphores. Data moves between devices by JAX's collectives and lax.ppermute only.
A program may use at most 64 MiB of HBM per device.

```python
import jax
import jax.numpy as jnp
import numpy as np
from jax import lax

ROWS_DEV = 512
VECS = 256
TILE = 128
NTILE = 4
ORDER = 262144
N_GRP = 8
N_SLAB = 64


def tile_mask(key):
    rows = ORDER // TILE
    slabs = rows // NTILE
    key_base, key_row, key_col = jax.random.split(key, 3)
    base = (jax.random.randint(key_base, (rows, NTILE), 0, 3) == 0).astype(jnp.int32)
    pick_row = jax.random.randint(key_row, (slabs, 1), 0, NTILE)
    pick_col = jax.random.randint(key_col, (slabs, 1), 0, NTILE)
    local_row = (jnp.arange(rows, dtype=jnp.int32) % NTILE).reshape(slabs, NTILE)
    row_hit = (local_row == pick_row).reshape(rows, 1)
    col_hit = jnp.arange(NTILE, dtype=jnp.int32).reshape(1, NTILE) == jnp.repeat(pick_col, NTILE, axis=0)
    forced = (row_hit & col_hit).astype(jnp.int32)
    return jnp.maximum(base, forced)


def draw_slab_mask(key, part):
    key = jax.random.fold_in(key, 11)
    return tile_mask(key)


def draw_grp_mask(key, part):
    key = jax.random.fold_in(key, 23)
    return tile_mask(key)


def shard_levels(key, dims, pieces, low, largest):
    level, own = 1.0, jax.random.fold_in(key, 6)
    for axis_at, parts in pieces:
        steps = jnp.exp(jax.random.uniform(jax.random.fold_in(own, axis_at), (parts,), jnp.float32, low / len(pieces), largest / len(pieces)))
        level = level * jnp.repeat(steps, dims[axis_at] // parts).reshape([-1 if axis == axis_at else 1 for axis in range(len(dims))])
    return level


def gaussian(key, extent, deviation, most, pieces=(), kind=jnp.bfloat16):
    factor_of = shard_levels(key, extent, pieces, -0.22, 0.18) if pieces else 1.0
    values = jax.random.normal(key, extent, jnp.float32) * deviation * factor_of
    return jnp.minimum(jnp.maximum(values, -most), most).astype(kind)


def setup_inputs(seed: int = 0) -> dict:
    splits = jax.random.split(jax.random.key(seed), 7)
    return {
        "vectors": gaussian(splits[0], (ORDER, VECS), 1.0, 6.0, ((0, 512),), jnp.float32),
        "diag_block": gaussian(splits[1], (ORDER, ROWS_DEV), ROWS_DEV ** -0.5, 0.25, ((0, 512),), jnp.float32),
        "slab_tiles": gaussian(splits[2], (ORDER, ROWS_DEV), (ROWS_DEV // 3) ** -0.5, 0.4375, ((0, 512),), jnp.float32),
        "slab_mask": draw_slab_mask(jax.random.fold_in(splits[6], 71), 0),
        "grp_tiles": gaussian(splits[4], (ORDER, ROWS_DEV), (ROWS_DEV // 3) ** -0.5, 0.4375, ((0, 512),), jnp.float32),
        "grp_mask": draw_grp_mask(jax.random.fold_in(splits[6], 71), 0),
    }


CENTER = 0.5
HALF_SPAN = 5.0


def expand(mask):
    full = jnp.repeat(jnp.repeat(mask.astype(jnp.float32), TILE, axis=0), TILE, axis=1)
    return full


def direct(block, vecs):
    return jnp.einsum("gsij,gsjk->gsik", block, vecs, precision=lax.Precision.HIGHEST)


def transposed(block, vecs):
    return jnp.einsum("gsji,gsjk->gsik", block, vecs, precision=lax.Precision.HIGHEST)


def reference(vectors, diag_block, slab_tiles, slab_mask, grp_tiles, grp_mask):
    shape4 = (N_GRP, N_SLAB, ROWS_DEV, ROWS_DEV)
    diag_sym = diag_block.reshape(shape4)
    diag_sym = 0.5 * (diag_sym + jnp.swapaxes(diag_sym, 2, 3))
    slab_block = (slab_tiles * expand(slab_mask)).reshape(shape4)
    grp_block = (grp_tiles * expand(grp_mask)).reshape(shape4)
    slab_perm = np.arange(N_SLAB) ^ (N_SLAB // 2)
    grp_perm = np.arange(N_GRP) ^ (N_GRP // 2)

    def apply(flat):
        vecs = flat.reshape(N_GRP, N_SLAB, ROWS_DEV, VECS)
        total = direct(diag_sym, vecs)
        total = total + direct(slab_block, vecs[:, slab_perm])
        total = total + transposed(slab_block, vecs)[:, slab_perm]
        total = total + direct(grp_block, vecs[grp_perm])
        total = total + transposed(grp_block, vecs)[grp_perm]
        return total.reshape(flat.shape)

    first = (apply(vectors) - CENTER * vectors) / HALF_SPAN
    return 2.0 * (apply(first) - CENTER * first) / HALF_SPAN - vectors
```

```python
import jax
import jax.numpy as jnp
from jax import lax
from jax.sharding import PartitionSpec as P

CENTER = 0.5
HALF_SPAN = 5.0


def expand(mask, width):
    return jnp.repeat(jnp.repeat(mask.astype(jnp.float32), width, axis=0), width, axis=1)


def direct(block, vecs):
    return jnp.dot(block, vecs, precision=lax.Precision.HIGH, preferred_element_type=jnp.float32)


def transposed(block, vecs):
    return lax.dot_general(
        block,
        vecs,
        (((0,), (0,)), ((), ())),
        precision=lax.Precision.HIGH,
        preferred_element_type=jnp.float32,
    )


def owns(slab, half):
    return (slab < half) == (slab % 2 == 0)


def body(vectors, diag_block, slab_tiles, slab_mask, grp_tiles, grp_mask):
    width = slab_tiles.shape[0] // slab_mask.shape[0]
    n_slab, n_grp = lax.axis_size("slab"), lax.axis_size("grp")
    half = n_slab // 2
    owner = owns(lax.axis_index("slab"), half)
    to_owner = [(i, i ^ half) for i in range(n_slab) if not owns(i, half)]
    from_owner = [(i, i ^ half) for i in range(n_slab) if owns(i, half)]
    grp_pairs = [(i, i ^ (n_grp // 2)) for i in range(n_grp)]

    slab_block = slab_tiles * expand(slab_mask, width)
    grp_block = grp_tiles * expand(grp_mask, width)

    vecs_in = lax.ppermute(vectors, "slab", to_owner)
    slab_in = lax.ppermute(slab_block, "slab", to_owner)
    vecs_grp = lax.ppermute(vectors, "grp", grp_pairs)
    grp_in = lax.ppermute(grp_block, "grp", grp_pairs)

    diag = 0.5 * (diag_block + diag_block.T) - CENTER * jnp.eye(diag_block.shape[0], dtype=jnp.float32)
    across = grp_block + grp_in.T
    base = direct(diag, vectors) + direct(across, vecs_grp)
    base_in = lax.ppermute(base, "slab", to_owner)

    pair = slab_block + slab_in.T
    back = transposed(pair, vectors)
    back_in = lax.ppermute(back, "slab", from_owner)
    first_own = (base + direct(pair, vecs_in)) / HALF_SPAN
    back2 = transposed(pair, first_own)
    back2_in = lax.ppermute(back2, "slab", from_owner)

    first = jnp.where(owner, first_own, (base + back_in) / HALF_SPAN)
    first_grp = lax.ppermute(first, "grp", grp_pairs)
    partner_first = (base_in + back) / HALF_SPAN
    cross = jnp.where(owner, direct(pair, partner_first), back2_in)
    total = direct(diag, first) + direct(across, first_grp) + cross
    return 2.0 * total / HALF_SPAN - vectors


def solution(mesh):
    spec = P(("grp", "slab"), None)
    return jax.shard_map(body, mesh=mesh, in_specs=(spec,) * 6, out_specs=spec, check_vma=False)
```

```python
import functools

import jax
import jax.numpy as jnp
from jax import lax
from jax.experimental import pallas as pl
from jax.experimental.pallas import tpu as pltpu
from jax.sharding import PartitionSpec as P

CENTER = 0.5
HALF_SPAN = 5.0
FIXED = 6
COST = 1000
GRP_CUTS = 2
BACK_CUTS = 1


def split(x):
    high = x.astype(jnp.bfloat16)
    return high, (x - high.astype(jnp.float32)).astype(jnp.bfloat16)


def product(a, b):
    dot = functools.partial(jnp.dot, preferred_element_type=jnp.float32)
    return dot(a[0], b[0]) + (dot(a[0], b[1]) + dot(a[1], b[0]))


def owns(slab, half):
    return (slab < half) == (slab % 2 == 0)


def pack_kernel(tile, slab_mask, grp_mask, slab_ref, grp_ref, fixed_ref, extra_ref, grp_out):
    n = slab_ref.shape[0] // tile
    fixed_ref[...] = jnp.zeros_like(fixed_ref)
    extra_ref[...] = jnp.zeros_like(extra_ref)
    slot = jnp.int32(0)
    for i in range(n):
        for j in range(n):
            at = (slice(i * tile, (i + 1) * tile), slice(j * tile, (j + 1) * tile))
            grp_out[at] = grp_ref[at] * grp_mask[i, j].astype(jnp.float32)
            stored = slab_mask[i, j] > 0

            @pl.when(jnp.logical_and(stored, slot < FIXED))
            def _():
                fixed_ref[slot] = slab_ref[at]

            @pl.when(jnp.logical_and(stored, slot >= FIXED))
            def _():
                extra_ref[slot - FIXED] = slab_ref[at]

            slot = slot + stored.astype(jnp.int32)


def pair_kernel(tile, own_mask, in_mask, own_ref, fixed_ref, extra_ref, vec_ref, out_ref, back_ref):
    n = own_ref.shape[0] // tile
    slot = jnp.int32(0)
    for i in range(n):
        for j in range(n):
            at = (slice(i * tile, (i + 1) * tile), slice(j * tile, (j + 1) * tile))
            out_ref[at] = own_ref[at] * own_mask[i, j].astype(jnp.float32)
    for i in range(n):
        for j in range(n):
            to = (slice(j * tile, (j + 1) * tile), slice(i * tile, (i + 1) * tile))
            stored = in_mask[i, j] > 0

            @pl.when(jnp.logical_and(stored, slot < FIXED))
            def _():
                out_ref[to] += fixed_ref[slot].T

            @pl.when(jnp.logical_and(stored, slot >= FIXED))
            def _():
                out_ref[to] += extra_ref[slot - FIXED].T

            slot = slot + stored.astype(jnp.int32)
    back_ref[...] = product(split(out_ref[...].T), split(vec_ref[...]))


def base_kernel(vec_ref, diag_ref, grp_ref, grp_in_ref, vec_grp_ref, base_ref, sym_ref, across_ref):
    raw = diag_ref[...]
    row = lax.broadcasted_iota(jnp.int32, raw.shape, 0)
    col = lax.broadcasted_iota(jnp.int32, raw.shape, 1)
    sym = 0.5 * (raw + raw.T) - jnp.where(row == col, jnp.float32(CENTER), jnp.float32(0))
    across = grp_ref[...] + grp_in_ref[...].T
    sym_ref[...] = sym
    across_ref[...] = across
    base_ref[...] = product(split(sym), split(vec_ref[...])) + product(split(across), split(vec_grp_ref[...]))


def first_kernel(base_ref, pair_ref, vec_in_ref, first_ref, back_ref):
    pair = pair_ref[...]
    first = (base_ref[...] + product(split(pair), split(vec_in_ref[...]))) / HALF_SPAN
    first_ref[...] = first
    back_ref[...] = product(split(pair.T), split(first))


def near_kernel(sym_ref, across_ref, first_ref, *refs):
    *first_grp_refs, near_ref = refs
    first_grp = jnp.concatenate([ref[...] for ref in first_grp_refs], axis=0)
    near_ref[...] = product(split(sym_ref[...]), split(first_ref[...])) + product(
        split(across_ref[...]), split(first_grp)
    )


def far_kernel(pair_ref, base_in_ref, back_ref, far_ref):
    first = (base_in_ref[...] + back_ref[...]) / HALF_SPAN
    far_ref[...] = product(split(pair_ref[...]), split(first))


def local_call(kernel, ins, out_shape):
    spaces = [pl.BlockSpec(memory_space=pltpu.SMEM if x.dtype == jnp.int32 else pltpu.VMEM) for x in ins]
    many = isinstance(out_shape, tuple)
    vmem = pl.BlockSpec(memory_space=pltpu.VMEM)
    return pl.pallas_call(
        kernel,
        out_shape=out_shape,
        in_specs=spaces,
        out_specs=(vmem,) * len(out_shape) if many else vmem,
        compiler_params=pltpu.CompilerParams(vmem_limit_bytes=24 * 1024 * 1024),
        cost_estimate=pl.CostEstimate(flops=COST, bytes_accessed=COST, transcendentals=0),
    )(*ins)


def body(vectors, diag_block, slab_tiles, slab_mask, grp_tiles, grp_mask):
    rows, n_tile = slab_tiles.shape[0], slab_mask.shape[0]
    tile = rows // n_tile
    slots = n_tile * n_tile
    n_slab, n_grp = lax.axis_size("slab"), lax.axis_size("grp")
    half = n_slab // 2
    owner = owns(lax.axis_index("slab"), half)
    to_owner = [(i, i ^ half) for i in range(n_slab) if not owns(i, half)]
    from_owner = [(i, i ^ half) for i in range(n_slab) if owns(i, half)]
    grp_pairs = [(i, i ^ (n_grp // 2)) for i in range(n_grp)]
    f32 = jnp.float32
    square = jax.ShapeDtypeStruct((rows, rows), f32)
    block = jax.ShapeDtypeStruct(vectors.shape, f32)

    vecs_grp = lax.ppermute(vectors, "grp", grp_pairs)
    vecs_in = lax.ppermute(vectors, "slab", to_owner)
    mask_in = lax.ppermute(slab_mask, "slab", to_owner)

    fixed, extra, grp_block = local_call(
        functools.partial(pack_kernel, tile),
        (slab_mask, grp_mask, slab_tiles, grp_tiles),
        (
            jax.ShapeDtypeStruct((FIXED, tile, tile), f32),
            jax.ShapeDtypeStruct((slots - FIXED, tile, tile), f32),
            square,
        ),
    )
    grp_in = lax.ppermute(grp_block, "grp", grp_pairs)
    fixed_in = lax.ppermute(fixed, "slab", to_owner)

    sizes = (0, 1, 2, 3, 4, 6, slots - FIXED)

    def send(k):
        def branch(tiles):
            if k == 0:
                return jnp.zeros_like(tiles)
            got = lax.ppermute(tiles[:k], "slab", to_owner)
            return jnp.concatenate([got, jnp.zeros((tiles.shape[0] - k, tile, tile), f32)], axis=0)

        return branch

    over = jnp.sum(jnp.where(owner, mask_in, slab_mask)) - FIXED
    which = sum((over > k).astype(jnp.int32) for k in sizes[:-1])
    extra_in = lax.switch(which, [send(k) for k in sizes], extra)

    base, sym, across = local_call(
        base_kernel, (vectors, diag_block, grp_block, grp_in, vecs_grp), (block, square, square)
    )
    base_in = lax.ppermute(base, "slab", to_owner)

    base, fixed_in, extra_in = lax.optimization_barrier((base, fixed_in, extra_in))
    pair, back = local_call(
        functools.partial(pair_kernel, tile),
        (slab_mask, mask_in, slab_tiles, fixed_in, extra_in, vectors),
        (square, block),
    )
    back_in = jnp.concatenate(
        [lax.ppermute(x, "slab", from_owner) for x in jnp.split(back, BACK_CUTS, axis=0)], axis=0
    )
    first_own, back2 = local_call(first_kernel, (base, pair, vecs_in), (block, block))
    back2_in = lax.ppermute(back2, "slab", from_owner)

    first = jnp.where(owner, first_own, (base + back_in) / HALF_SPAN)
    first_grp = [lax.ppermute(x, "grp", grp_pairs) for x in jnp.split(first, GRP_CUTS, axis=0)]
    far = local_call(far_kernel, (pair, base_in, back), block)
    near = local_call(near_kernel, (sym, across, first, *first_grp), block)
    total = near + jnp.where(owner, far, back2_in)
    return 2.0 * total / HALF_SPAN - vectors


def solution(mesh):
    spec = P(("grp", "slab"), None)
    return jax.shard_map(body, mesh=mesh, in_specs=(spec,) * 6, out_specs=spec, check_vma=False)
```

```python
import functools

import jax
import jax.numpy as jnp
from jax import lax
from jax.experimental import pallas as pl
from jax.experimental.pallas import tpu as pltpu
from jax.sharding import PartitionSpec as P

CENTER = 0.5
HALF_SPAN = 5.0
PIECE = 2
PIECES = 3
FIXED = PIECE * PIECES
COST = 1000
GRP_CUTS = 2
BACK_CUTS = 1


def split(x):
    high = x.astype(jnp.bfloat16)
    return high, (x - high.astype(jnp.float32)).astype(jnp.bfloat16)


def product(a, b):
    dot = functools.partial(jnp.dot, preferred_element_type=jnp.float32)
    return dot(a[0], b[0]) + (dot(a[0], b[1]) + dot(a[1], b[0]))


def owns(slab, half):
    return (slab < half) == (slab % 2 == 0)


def pack_kernel(tile, slab_mask, grp_mask, slab_ref, grp_ref, *out_refs):
    *slot_refs, grp_out = out_refs
    n = slab_ref.shape[0] // tile
    for ref in slot_refs:
        ref[...] = jnp.zeros_like(ref)
    slot = jnp.int32(0)
    for i in range(n):
        for j in range(n):
            at = (slice(i * tile, (i + 1) * tile), slice(j * tile, (j + 1) * tile))
            grp_out[at] = grp_ref[at] * grp_mask[i, j].astype(jnp.float32)
            stored, first = slab_mask[i, j] > 0, 0
            for ref in slot_refs:
                inside = jnp.logical_and(slot >= first, slot < first + ref.shape[0])

                @pl.when(jnp.logical_and(stored, inside))
                def _():
                    ref[slot - first] = slab_ref[at]

                first += ref.shape[0]
            slot = slot + stored.astype(jnp.int32)


def pair_kernel(tile, own_mask, in_mask, own_ref, vec_ref, *refs):
    *slot_refs, out_ref, back_ref = refs
    n = own_ref.shape[0] // tile
    slot = jnp.int32(0)
    for i in range(n):
        for j in range(n):
            at = (slice(i * tile, (i + 1) * tile), slice(j * tile, (j + 1) * tile))
            out_ref[at] = own_ref[at] * own_mask[i, j].astype(jnp.float32)
    for i in range(n):
        for j in range(n):
            to = (slice(j * tile, (j + 1) * tile), slice(i * tile, (i + 1) * tile))
            stored, first = in_mask[i, j] > 0, 0
            for ref in slot_refs:
                inside = jnp.logical_and(slot >= first, slot < first + ref.shape[0])

                @pl.when(jnp.logical_and(stored, inside))
                def _():
                    out_ref[to] += ref[slot - first].T

                first += ref.shape[0]
            slot = slot + stored.astype(jnp.int32)
    back_ref[...] = product(split(out_ref[...].T), split(vec_ref[...]))


def base_kernel(vec_ref, diag_ref, grp_ref, grp_in_ref, vec_grp_ref, base_ref, sym_ref, across_ref):
    raw = diag_ref[...]
    row = lax.broadcasted_iota(jnp.int32, raw.shape, 0)
    col = lax.broadcasted_iota(jnp.int32, raw.shape, 1)
    sym = 0.5 * (raw + raw.T) - jnp.where(row == col, jnp.float32(CENTER), jnp.float32(0))
    across = grp_ref[...] + grp_in_ref[...].T
    sym_ref[...] = sym
    across_ref[...] = across
    base_ref[...] = product(split(sym), split(vec_ref[...])) + product(split(across), split(vec_grp_ref[...]))


def first_kernel(base_ref, pair_ref, vec_in_ref, first_ref, back_ref):
    pair = pair_ref[...]
    first = (base_ref[...] + product(split(pair), split(vec_in_ref[...]))) / HALF_SPAN
    first_ref[...] = first
    back_ref[...] = product(split(pair.T), split(first))


def near_kernel(sym_ref, across_ref, first_ref, *refs):
    *first_grp_refs, near_ref = refs
    first_grp = jnp.concatenate([ref[...] for ref in first_grp_refs], axis=0)
    near_ref[...] = product(split(sym_ref[...]), split(first_ref[...])) + product(
        split(across_ref[...]), split(first_grp)
    )


def far_kernel(pair_ref, base_in_ref, back_ref, far_ref):
    first = (base_in_ref[...] + back_ref[...]) / HALF_SPAN
    far_ref[...] = product(split(pair_ref[...]), split(first))


def local_call(kernel, ins, out_shape):
    spaces = [pl.BlockSpec(memory_space=pltpu.SMEM if x.dtype == jnp.int32 else pltpu.VMEM) for x in ins]
    many = isinstance(out_shape, tuple)
    vmem = pl.BlockSpec(memory_space=pltpu.VMEM)
    return pl.pallas_call(
        kernel,
        out_shape=out_shape,
        in_specs=spaces,
        out_specs=(vmem,) * len(out_shape) if many else vmem,
        compiler_params=pltpu.CompilerParams(vmem_limit_bytes=24 * 1024 * 1024),
        cost_estimate=pl.CostEstimate(flops=COST, bytes_accessed=COST, transcendentals=0),
    )(*ins)


def body(vectors, diag_block, slab_tiles, slab_mask, grp_tiles, grp_mask):
    rows, n_tile = slab_tiles.shape[0], slab_mask.shape[0]
    tile = rows // n_tile
    slots = n_tile * n_tile
    n_slab, n_grp = lax.axis_size("slab"), lax.axis_size("grp")
    half = n_slab // 2
    owner = owns(lax.axis_index("slab"), half)
    to_owner = [(i, i ^ half) for i in range(n_slab) if not owns(i, half)]
    from_owner = [(i, i ^ half) for i in range(n_slab) if owns(i, half)]
    grp_pairs = [(i, i ^ (n_grp // 2)) for i in range(n_grp)]
    f32 = jnp.float32
    square = jax.ShapeDtypeStruct((rows, rows), f32)
    block = jax.ShapeDtypeStruct(vectors.shape, f32)

    vecs_grp = lax.ppermute(vectors, "grp", grp_pairs)
    vecs_in = lax.ppermute(vectors, "slab", to_owner)
    mask_in = lax.ppermute(slab_mask, "slab", to_owner)

    *fixed, extra, grp_block = local_call(
        functools.partial(pack_kernel, tile),
        (slab_mask, grp_mask, slab_tiles, grp_tiles),
        (
            *[jax.ShapeDtypeStruct((PIECE, tile, tile), f32)] * PIECES,
            jax.ShapeDtypeStruct((slots - FIXED, tile, tile), f32),
            square,
        ),
    )
    grp_in = lax.ppermute(grp_block, "grp", grp_pairs)
    fixed_in = [lax.ppermute(x, "slab", to_owner) for x in fixed]

    sizes = (0, 1, 2, 3, 4, 5, 6, 8, slots - FIXED)

    def send(k):
        def branch(tiles):
            if k == 0:
                return jnp.zeros_like(tiles)
            got = lax.ppermute(tiles[:k], "slab", to_owner)
            return jnp.concatenate([got, jnp.zeros((tiles.shape[0] - k, tile, tile), f32)], axis=0)

        return branch

    over = jnp.sum(jnp.where(owner, mask_in, slab_mask)) - FIXED
    which = sum((over > k).astype(jnp.int32) for k in sizes[:-1])
    extra_in = lax.switch(which, [send(k) for k in sizes], extra)

    base, sym, across = local_call(
        base_kernel, (vectors, diag_block, grp_block, grp_in, vecs_grp), (block, square, square)
    )
    base_in = lax.ppermute(base, "slab", to_owner)

    base, fixed_in, extra_in = lax.optimization_barrier((base, fixed_in, extra_in))
    pair, back = local_call(
        functools.partial(pair_kernel, tile),
        (slab_mask, mask_in, slab_tiles, vectors, *fixed_in, extra_in),
        (square, block),
    )
    back_in = jnp.concatenate(
        [lax.ppermute(x, "slab", from_owner) for x in jnp.split(back, BACK_CUTS, axis=0)], axis=0
    )
    first_own, back2 = local_call(first_kernel, (base, pair, vecs_in), (block, block))
    back2_in = lax.ppermute(back2, "slab", from_owner)

    first = jnp.where(owner, first_own, (base + back_in) / HALF_SPAN)
    first_grp = [lax.ppermute(x, "grp", grp_pairs) for x in jnp.split(first, GRP_CUTS, axis=0)]
    far = local_call(far_kernel, (pair, base_in, back), block)
    near = local_call(near_kernel, (sym, across, first, *first_grp), block)
    total = near + jnp.where(owner, far, back2_in)
    return 2.0 * total / HALF_SPAN - vectors


def solution(mesh):
    spec = P(("grp", "slab"), None)
    return jax.shard_map(body, mesh=mesh, in_specs=(spec,) * 6, out_specs=spec, check_vma=False)
```

```python
import functools

import jax
import jax.numpy as jnp
from jax import lax
from jax.experimental import pallas as pl
from jax.experimental.pallas import tpu as pltpu
from jax.sharding import PartitionSpec as P

CENTER = 0.5
HALF_SPAN = 5.0
PIECE = 6
PIECES = 1
FIXED = PIECE * PIECES
COST = 1000
GRP_CUTS = 2
BACK_CUTS = 1


def split(x):
    high = x.astype(jnp.bfloat16)
    return high, (x - high.astype(jnp.float32)).astype(jnp.bfloat16)


def product(a, b):
    dot = functools.partial(jnp.dot, preferred_element_type=jnp.float32)
    return dot(a[0], b[0]) + (dot(a[0], b[1]) + dot(a[1], b[0]))


def owns(slab, half):
    return (slab < half) == (slab % 2 == 0)


def pack_kernel(tile, slab_mask, grp_mask, slab_ref, grp_ref, *out_refs):
    *slot_refs, grp_out = out_refs
    n = slab_ref.shape[0] // tile
    for ref in slot_refs:
        ref[...] = jnp.zeros_like(ref)
    slot = jnp.int32(0)
    for i in range(n):
        for j in range(n):
            at = (slice(i * tile, (i + 1) * tile), slice(j * tile, (j + 1) * tile))
            grp_out[at] = grp_ref[at] * grp_mask[i, j].astype(jnp.float32)
            stored, first = slab_mask[i, j] > 0, 0
            for ref in slot_refs:
                inside = jnp.logical_and(slot >= first, slot < first + ref.shape[0])

                @pl.when(jnp.logical_and(stored, inside))
                def _():
                    ref[slot - first] = slab_ref[at]

                first += ref.shape[0]
            slot = slot + stored.astype(jnp.int32)


def pair_kernel(tile, own_mask, in_mask, own_ref, vec_ref, *refs):
    *slot_refs, out_ref, back_ref = refs
    n = own_ref.shape[0] // tile
    slot = jnp.int32(0)
    for i in range(n):
        for j in range(n):
            at = (slice(i * tile, (i + 1) * tile), slice(j * tile, (j + 1) * tile))
            out_ref[at] = own_ref[at] * own_mask[i, j].astype(jnp.float32)
    for i in range(n):
        for j in range(n):
            to = (slice(j * tile, (j + 1) * tile), slice(i * tile, (i + 1) * tile))
            stored, first = in_mask[i, j] > 0, 0
            for ref in slot_refs:
                inside = jnp.logical_and(slot >= first, slot < first + ref.shape[0])

                @pl.when(jnp.logical_and(stored, inside))
                def _():
                    out_ref[to] += ref[slot - first].T

                first += ref.shape[0]
            slot = slot + stored.astype(jnp.int32)
    back_ref[...] = product(split(out_ref[...].T), split(vec_ref[...]))


def base_kernel(
    vec_ref, diag_ref, grp_ref, grp_in_ref, vec_grp_ref, vec_in_ref, base_ref, sym_ref, across_ref, high_ref, low_ref
):
    high_ref[...], low_ref[...] = split(vec_in_ref[...])
    raw = diag_ref[...]
    row = lax.broadcasted_iota(jnp.int32, raw.shape, 0)
    col = lax.broadcasted_iota(jnp.int32, raw.shape, 1)
    sym = 0.5 * (raw + raw.T) - jnp.where(row == col, jnp.float32(CENTER), jnp.float32(0))
    across = grp_ref[...] + grp_in_ref[...].T
    sym_ref[...] = sym
    across_ref[...] = across
    base_ref[...] = product(split(sym), split(vec_ref[...])) + product(split(across), split(vec_grp_ref[...]))


def first_kernel(base_ref, pair_ref, high_ref, low_ref, base_in_ref, back_ref, first_ref, back2_ref, far_ref):
    pair = split(pair_ref[...])
    first = (base_ref[...] + product(pair, (high_ref[...], low_ref[...]))) / HALF_SPAN
    first_ref[...] = first
    back2_ref[...] = product(split(pair_ref[...].T), split(first))
    far_ref[...] = product(pair, split((base_in_ref[...] + back_ref[...]) / HALF_SPAN))


def near_kernel(sym_ref, across_ref, first_ref, *refs):
    *first_grp_refs, near_ref = refs
    first_grp = jnp.concatenate([ref[...] for ref in first_grp_refs], axis=0)
    near_ref[...] = product(split(sym_ref[...]), split(first_ref[...])) + product(
        split(across_ref[...]), split(first_grp)
    )


def local_call(kernel, ins, out_shape):
    spaces = [pl.BlockSpec(memory_space=pltpu.SMEM if x.dtype == jnp.int32 else pltpu.VMEM) for x in ins]
    many = isinstance(out_shape, tuple)
    vmem = pl.BlockSpec(memory_space=pltpu.VMEM)
    return pl.pallas_call(
        kernel,
        out_shape=out_shape,
        in_specs=spaces,
        out_specs=(vmem,) * len(out_shape) if many else vmem,
        compiler_params=pltpu.CompilerParams(vmem_limit_bytes=24 * 1024 * 1024),
        cost_estimate=pl.CostEstimate(flops=COST, bytes_accessed=COST, transcendentals=0),
    )(*ins)


def body(vectors, diag_block, slab_tiles, slab_mask, grp_tiles, grp_mask):
    rows, n_tile = slab_tiles.shape[0], slab_mask.shape[0]
    tile = rows // n_tile
    slots = n_tile * n_tile
    n_slab, n_grp = lax.axis_size("slab"), lax.axis_size("grp")
    half = n_slab // 2
    owner = owns(lax.axis_index("slab"), half)
    to_owner = [(i, i ^ half) for i in range(n_slab) if not owns(i, half)]
    from_owner = [(i, i ^ half) for i in range(n_slab) if owns(i, half)]
    grp_pairs = [(i, i ^ (n_grp // 2)) for i in range(n_grp)]
    f32 = jnp.float32
    square = jax.ShapeDtypeStruct((rows, rows), f32)
    block = jax.ShapeDtypeStruct(vectors.shape, f32)

    vecs_grp = lax.ppermute(vectors, "grp", grp_pairs)
    vecs_in = lax.ppermute(vectors, "slab", to_owner)
    mask_in = lax.ppermute(slab_mask, "slab", to_owner)

    *fixed, extra, grp_block = local_call(
        functools.partial(pack_kernel, tile),
        (slab_mask, grp_mask, slab_tiles, grp_tiles),
        (
            *[jax.ShapeDtypeStruct((PIECE, tile, tile), f32)] * PIECES,
            jax.ShapeDtypeStruct((slots - FIXED, tile, tile), f32),
            square,
        ),
    )
    grp_in = lax.ppermute(grp_block, "grp", grp_pairs)
    fixed_in = [lax.ppermute(x, "slab", to_owner) for x in fixed]

    half_block = jax.ShapeDtypeStruct(vectors.shape, jnp.bfloat16)
    base, sym, across, high, low = local_call(
        base_kernel,
        (vectors, diag_block, grp_block, grp_in, vecs_grp, vecs_in),
        (block, square, square, half_block, half_block),
    )
    base_in = lax.ppermute(base, "slab", to_owner)

    sizes = (0, 1, 2, 3, 4, 6, slots - FIXED)

    def send(k):
        def branch(tiles):
            if k == 0:
                return jnp.zeros_like(tiles)
            got = lax.ppermute(tiles[:k], "slab", to_owner)
            return jnp.concatenate([got, jnp.zeros((tiles.shape[0] - k, tile, tile), f32)], axis=0)

        return branch

    extra, mask_in, base = lax.optimization_barrier((extra, mask_in, base))
    over = jnp.sum(jnp.where(owner, mask_in, slab_mask)) - FIXED
    which = sum((over > k).astype(jnp.int32) for k in sizes[:-1])
    extra_in = lax.switch(which, [send(k) for k in sizes], extra)

    pair, back = local_call(
        functools.partial(pair_kernel, tile),
        (slab_mask, mask_in, slab_tiles, vectors, *fixed_in, extra_in),
        (square, block),
    )
    back_in = lax.ppermute(back, "slab", from_owner)
    first_own, back2, far = local_call(
        first_kernel, (base, pair, high, low, base_in, back), (block, block, block)
    )
    back2_in = lax.ppermute(back2, "slab", from_owner)

    first = jnp.where(owner, first_own, (base + back_in) / HALF_SPAN)
    first_grp = [lax.ppermute(x, "grp", grp_pairs) for x in jnp.split(first, GRP_CUTS, axis=0)]
    near = local_call(near_kernel, (sym, across, first, *first_grp), block)
    total = near + jnp.where(owner, far, back2_in)
    return 2.0 * total / HALF_SPAN - vectors


def solution(mesh):
    spec = P(("grp", "slab"), None)
    return jax.shard_map(body, mesh=mesh, in_specs=(spec,) * 6, out_specs=spec, check_vma=False)
```

```python
import functools

import jax
import jax.numpy as jnp
from jax import lax
from jax.experimental import pallas as pl
from jax.experimental.pallas import tpu as pltpu
from jax.sharding import PartitionSpec as P

CENTER = 0.5
HALF_SPAN = 5.0
FIXED = 12
COST = 1000
GRP_CUTS = 1


def split(x):
    high = x.astype(jnp.bfloat16)
    return high, (x - high.astype(jnp.float32)).astype(jnp.bfloat16)


def product(a, b):
    dot = functools.partial(jnp.dot, preferred_element_type=jnp.float32)
    return dot(a[0], b[0]) + (dot(a[0], b[1]) + dot(a[1], b[0]))


def owns(slab, half):
    return (slab < half) == (slab % 2 == 0)


def pack_kernel(tile, slab_mask, slab_ref, bulk_ref, extra_ref):
    n = slab_ref.shape[0] // tile
    bulk_ref[...] = jnp.zeros_like(bulk_ref)
    extra_ref[...] = jnp.zeros_like(extra_ref)
    tail = (bulk_ref.shape[0] - FIXED * tile, tile)
    row, col = lax.broadcasted_iota(jnp.int32, tail, 0), lax.broadcasted_iota(jnp.int32, tail, 1)
    mask = jnp.zeros(tail, jnp.float32)
    slot = jnp.int32(0)
    for i in range(n):
        for j in range(n):
            at = (slice(i * tile, (i + 1) * tile), slice(j * tile, (j + 1) * tile))
            stored = slab_mask[i, j] > 0
            mask = jnp.where(jnp.logical_and(row == i, col == j), slab_mask[i, j].astype(jnp.float32), mask)

            @pl.when(jnp.logical_and(stored, slot < FIXED))
            def _():
                bulk_ref[pl.ds(pl.multiple_of(slot * tile, tile), tile), :] = slab_ref[at]

            @pl.when(jnp.logical_and(stored, slot >= FIXED))
            def _():
                extra_ref[slot - FIXED] = slab_ref[at]

            slot = slot + stored.astype(jnp.int32)
    bulk_ref[FIXED * tile :, :] = mask


def masked_kernel(tile, mask, tiles_ref, *out_refs):
    n = tiles_ref.shape[0] // tile
    for i in range(n):
        out_ref = out_refs[i * len(out_refs) // n]
        top = i * tile % out_ref.shape[0]
        for j in range(n):
            cols = slice(j * tile, (j + 1) * tile)
            out_ref[top : top + tile, cols] = tiles_ref[i * tile : (i + 1) * tile, cols] * mask[i, j].astype(jnp.float32)


def pair_kernel(tile, own_mask, in_mask, own_ref, bulk_ref, extra_ref, vec_ref, out_ref, back_ref):
    n = own_ref.shape[0] // tile
    for i in range(n):
        for j in range(n):
            at = (slice(i * tile, (i + 1) * tile), slice(j * tile, (j + 1) * tile))
            out_ref[at] = own_ref[at] * own_mask[i, j].astype(jnp.float32)
    slot = jnp.int32(0)
    for i in range(n):
        for j in range(n):
            to = (slice(j * tile, (j + 1) * tile), slice(i * tile, (i + 1) * tile))
            stored = in_mask[i, j] > 0

            @pl.when(jnp.logical_and(stored, slot < FIXED))
            def _():
                out_ref[to] += bulk_ref[pl.ds(pl.multiple_of(slot * tile, tile), tile), :].T

            @pl.when(jnp.logical_and(stored, slot >= FIXED))
            def _():
                out_ref[to] += extra_ref[slot - FIXED].T

            slot = slot + stored.astype(jnp.int32)
    back_ref[...] = product(split(out_ref[...].T), split(vec_ref[...]))


def base_kernel(vec_ref, diag_ref, vec_grp_ref, *refs):
    *grp_refs, base_ref, sym_ref, across_ref = refs
    half = len(grp_refs) // 2
    grp, grp_in = (jnp.concatenate([ref[...] for ref in part], axis=0) for part in (grp_refs[:half], grp_refs[half:]))
    raw = diag_ref[...]
    row = lax.broadcasted_iota(jnp.int32, raw.shape, 0)
    col = lax.broadcasted_iota(jnp.int32, raw.shape, 1)
    sym = 0.5 * (raw + raw.T) - jnp.where(row == col, jnp.float32(CENTER), jnp.float32(0))
    across = grp + grp_in.T
    sym_ref[...] = sym
    across_ref[...] = across
    base_ref[...] = product(split(sym), split(vec_ref[...])) + product(split(across), split(vec_grp_ref[...]))


def first_kernel(base_ref, pair_ref, vec_in_ref, first_ref, back_ref):
    pair = pair_ref[...]
    first = (base_ref[...] + product(split(pair), split(vec_in_ref[...]))) / HALF_SPAN
    first_ref[...] = first
    back_ref[...] = product(split(pair.T), split(first))


def near_kernel(sym_ref, across_ref, first_ref, *refs):
    *first_grp_refs, near_ref = refs
    first_grp = jnp.concatenate([ref[...] for ref in first_grp_refs], axis=0)
    near_ref[...] = product(split(sym_ref[...]), split(first_ref[...])) + product(
        split(across_ref[...]), split(first_grp)
    )


def far_kernel(pair_ref, base_in_ref, back_ref, far_ref):
    first = (base_in_ref[...] + back_ref[...]) / HALF_SPAN
    far_ref[...] = product(split(pair_ref[...]), split(first))


def local_call(kernel, ins, out_shape):
    spaces = [pl.BlockSpec(memory_space=pltpu.SMEM if x.dtype == jnp.int32 else pltpu.VMEM) for x in ins]
    many = isinstance(out_shape, tuple)
    vmem = pl.BlockSpec(memory_space=pltpu.VMEM)
    return pl.pallas_call(
        kernel,
        out_shape=out_shape,
        in_specs=spaces,
        out_specs=(vmem,) * len(out_shape) if many else vmem,
        compiler_params=pltpu.CompilerParams(vmem_limit_bytes=24 * 1024 * 1024),
        cost_estimate=pl.CostEstimate(flops=COST, bytes_accessed=COST, transcendentals=0),
    )(*ins)


def body(vectors, diag_block, slab_tiles, slab_mask, grp_tiles, grp_mask):
    rows, n_tile = slab_tiles.shape[0], slab_mask.shape[0]
    tile = rows // n_tile
    slots = n_tile * n_tile
    n_slab, n_grp = lax.axis_size("slab"), lax.axis_size("grp")
    half = n_slab // 2
    owner = owns(lax.axis_index("slab"), half)
    to_owner = [(i, i ^ half) for i in range(n_slab) if not owns(i, half)]
    from_owner = [(i, i ^ half) for i in range(n_slab) if owns(i, half)]
    grp_pairs = [(i, i ^ (n_grp // 2)) for i in range(n_grp)]
    f32 = jnp.float32
    square = jax.ShapeDtypeStruct((rows, rows), f32)
    block = jax.ShapeDtypeStruct(vectors.shape, f32)

    vecs_grp = lax.ppermute(vectors, "grp", grp_pairs)
    vecs_in = lax.ppermute(vectors, "slab", to_owner)

    bulk, extra = local_call(
        functools.partial(pack_kernel, tile),
        (slab_mask, slab_tiles),
        (
            jax.ShapeDtypeStruct((FIXED * tile + 8, tile), f32),
            jax.ShapeDtypeStruct((slots - FIXED, tile, tile), f32),
        ),
    )
    bulk_in = lax.ppermute(bulk, "slab", to_owner)
    grp_blocks = local_call(
        functools.partial(masked_kernel, tile),
        (grp_mask, grp_tiles),
        (jax.ShapeDtypeStruct((rows // GRP_CUTS, rows), f32),) * GRP_CUTS,
    )
    grp_in = [lax.ppermute(x, "grp", grp_pairs) for x in grp_blocks]

    base, sym, across = local_call(
        base_kernel, (vectors, diag_block, vecs_grp, *grp_blocks, *grp_in), (block, square, square)
    )
    base_in = lax.ppermute(base, "slab", to_owner)

    base, bulk_in = lax.optimization_barrier((base, bulk_in))
    mask_in = bulk_in[FIXED * tile : FIXED * tile + n_tile, :n_tile].astype(jnp.int32)
    sizes = (0, slots - FIXED)

    def send(k):
        def branch(tiles):
            if k == 0:
                return jnp.zeros_like(tiles)
            return lax.ppermute(tiles, "slab", to_owner)

        return branch

    over = jnp.sum(jnp.where(owner, mask_in, slab_mask)) - FIXED
    which = sum((over > k).astype(jnp.int32) for k in sizes[:-1])
    extra_in = lax.switch(which, [send(k) for k in sizes], extra)

    pair, back = local_call(
        functools.partial(pair_kernel, tile),
        (slab_mask, mask_in, slab_tiles, bulk_in, extra_in, vectors),
        (square, block),
    )
    back_in = lax.ppermute(back, "slab", from_owner)
    first_own, back2 = local_call(first_kernel, (base, pair, vecs_in), (block, block))
    back2_in = lax.ppermute(back2, "slab", from_owner)

    far = local_call(far_kernel, (pair, base_in, back), block)
    far, back_in = lax.optimization_barrier((far, back_in))
    first = jnp.where(owner, first_own, (base + back_in) / HALF_SPAN)
    first_grp = [lax.ppermute(x, "grp", grp_pairs) for x in jnp.split(first, 2, axis=0)]
    near = local_call(near_kernel, (sym, across, first, *first_grp), block)
    total = near + jnp.where(owner, far, back2_in)
    return 2.0 * total / HALF_SPAN - vectors


def solution(mesh):
    spec = P(("grp", "slab"), None)
    return jax.shard_map(body, mesh=mesh, in_specs=(spec,) * 6, out_specs=spec, check_vma=False)
```

```python
import functools

import jax
import jax.numpy as jnp
from jax import lax
from jax.experimental import pallas as pl
from jax.experimental.pallas import tpu as pltpu
from jax.sharding import PartitionSpec as P

CENTER = 0.5
HALF_SPAN = 5.0
FIXED = 12
COST = 1000
GRP_CUTS = 2


def split(x):
    high = x.astype(jnp.bfloat16)
    return high, (x - high.astype(jnp.float32)).astype(jnp.bfloat16)


def product(a, b):
    dot = functools.partial(jnp.dot, preferred_element_type=jnp.float32)
    return dot(a[0], b[0]) + (dot(a[0], b[1]) + dot(a[1], b[0]))


def owns(slab, half):
    return (slab < half) == (slab % 2 == 0)


def pack_kernel(tile, slab_mask, slab_ref, bulk_ref, extra_ref):
    n = slab_ref.shape[0] // tile
    bulk_ref[...] = jnp.zeros_like(bulk_ref)
    extra_ref[...] = jnp.zeros_like(extra_ref)
    tail = (bulk_ref.shape[0] - FIXED * tile, tile)
    row, col = lax.broadcasted_iota(jnp.int32, tail, 0), lax.broadcasted_iota(jnp.int32, tail, 1)
    mask = jnp.zeros(tail, jnp.float32)
    slot = jnp.int32(0)
    for i in range(n):
        for j in range(n):
            at = (slice(i * tile, (i + 1) * tile), slice(j * tile, (j + 1) * tile))
            stored = slab_mask[i, j] > 0
            mask = jnp.where(jnp.logical_and(row == i, col == j), slab_mask[i, j].astype(jnp.float32), mask)

            @pl.when(jnp.logical_and(stored, slot < FIXED))
            def _():
                bulk_ref[pl.ds(pl.multiple_of(slot * tile, tile), tile), :] = slab_ref[at]

            @pl.when(jnp.logical_and(stored, slot >= FIXED))
            def _():
                extra_ref[slot - FIXED] = slab_ref[at]

            slot = slot + stored.astype(jnp.int32)
    bulk_ref[FIXED * tile :, :] = mask


def masked_kernel(tile, mask, tiles_ref, *out_refs):
    n = tiles_ref.shape[0] // tile
    for i in range(n):
        out_ref = out_refs[i * len(out_refs) // n]
        top = i * tile % out_ref.shape[0]
        for j in range(n):
            cols = slice(j * tile, (j + 1) * tile)
            out_ref[top : top + tile, cols] = tiles_ref[i * tile : (i + 1) * tile, cols] * mask[i, j].astype(jnp.float32)


def pair_kernel(tile, own_mask, in_mask, own_ref, bulk_ref, extra_ref, vec_ref, out_ref, back_ref):
    n = own_ref.shape[0] // tile
    for i in range(n):
        for j in range(n):
            at = (slice(i * tile, (i + 1) * tile), slice(j * tile, (j + 1) * tile))
            out_ref[at] = own_ref[at] * own_mask[i, j].astype(jnp.float32)
    slot = jnp.int32(0)
    for i in range(n):
        for j in range(n):
            to = (slice(j * tile, (j + 1) * tile), slice(i * tile, (i + 1) * tile))
            stored = in_mask[i, j] > 0

            @pl.when(jnp.logical_and(stored, slot < FIXED))
            def _():
                out_ref[to] += bulk_ref[pl.ds(pl.multiple_of(slot * tile, tile), tile), :].T

            @pl.when(jnp.logical_and(stored, slot >= FIXED))
            def _():
                out_ref[to] += extra_ref[slot - FIXED].T

            slot = slot + stored.astype(jnp.int32)
    back_ref[...] = product(split(out_ref[...].T), split(vec_ref[...]))


def base_kernel(vec_ref, diag_ref, vec_grp_ref, *refs):
    *grp_refs, base_ref, sym_ref, across_ref = refs
    half = len(grp_refs) // 2
    grp, grp_in = (jnp.concatenate([ref[...] for ref in part], axis=0) for part in (grp_refs[:half], grp_refs[half:]))
    raw = diag_ref[...]
    row = lax.broadcasted_iota(jnp.int32, raw.shape, 0)
    col = lax.broadcasted_iota(jnp.int32, raw.shape, 1)
    sym = 0.5 * (raw + raw.T) - jnp.where(row == col, jnp.float32(CENTER), jnp.float32(0))
    across = grp + grp_in.T
    sym_ref[...] = sym
    across_ref[...] = across
    base_ref[...] = product(split(sym), split(vec_ref[...])) + product(split(across), split(vec_grp_ref[...]))


def first_kernel(base_ref, pair_ref, vec_in_ref, first_ref, back_ref):
    pair = pair_ref[...]
    first = (base_ref[...] + product(split(pair), split(vec_in_ref[...]))) / HALF_SPAN
    first_ref[...] = first
    back_ref[...] = product(split(pair.T), split(first))


def near_kernel(sym_ref, across_ref, first_ref, *refs):
    *first_grp_refs, near_ref = refs
    first_grp = jnp.concatenate([ref[...] for ref in first_grp_refs], axis=0)
    near_ref[...] = product(split(sym_ref[...]), split(first_ref[...])) + product(
        split(across_ref[...]), split(first_grp)
    )


def far_kernel(pair_ref, base_in_ref, back_ref, far_ref):
    first = (base_in_ref[...] + back_ref[...]) / HALF_SPAN
    far_ref[...] = product(split(pair_ref[...]), split(first))


def local_call(kernel, ins, out_shape):
    spaces = [pl.BlockSpec(memory_space=pltpu.SMEM if x.dtype == jnp.int32 else pltpu.VMEM) for x in ins]
    many = isinstance(out_shape, tuple)
    vmem = pl.BlockSpec(memory_space=pltpu.VMEM)
    return pl.pallas_call(
        kernel,
        out_shape=out_shape,
        in_specs=spaces,
        out_specs=(vmem,) * len(out_shape) if many else vmem,
        compiler_params=pltpu.CompilerParams(vmem_limit_bytes=24 * 1024 * 1024),
        cost_estimate=pl.CostEstimate(flops=COST, bytes_accessed=COST, transcendentals=0),
    )(*ins)


def body(vectors, diag_block, slab_tiles, slab_mask, grp_tiles, grp_mask):
    rows, n_tile = slab_tiles.shape[0], slab_mask.shape[0]
    tile = rows // n_tile
    slots = n_tile * n_tile
    n_slab, n_grp = lax.axis_size("slab"), lax.axis_size("grp")
    half = n_slab // 2
    owner = owns(lax.axis_index("slab"), half)
    to_owner = [(i, i ^ half) for i in range(n_slab) if not owns(i, half)]
    from_owner = [(i, i ^ half) for i in range(n_slab) if owns(i, half)]
    grp_pairs = [(i, i ^ (n_grp // 2)) for i in range(n_grp)]
    f32 = jnp.float32
    square = jax.ShapeDtypeStruct((rows, rows), f32)
    block = jax.ShapeDtypeStruct(vectors.shape, f32)

    vecs_grp = lax.ppermute(vectors, "grp", grp_pairs)
    vecs_in = lax.ppermute(vectors, "slab", to_owner)

    bulk, extra = local_call(
        functools.partial(pack_kernel, tile),
        (slab_mask, slab_tiles),
        (
            jax.ShapeDtypeStruct((FIXED * tile + 8, tile), f32),
            jax.ShapeDtypeStruct((slots - FIXED, tile, tile), f32),
        ),
    )
    bulk_in = lax.ppermute(bulk, "slab", to_owner)
    grp_blocks = local_call(
        functools.partial(masked_kernel, tile),
        (grp_mask, grp_tiles),
        (jax.ShapeDtypeStruct((rows // GRP_CUTS, rows), f32),) * GRP_CUTS,
    )
    grp_in = [lax.ppermute(x, "grp", grp_pairs) for x in grp_blocks]

    base, sym, across = local_call(
        base_kernel, (vectors, diag_block, vecs_grp, *grp_blocks, *grp_in), (block, square, square)
    )
    base_in = lax.ppermute(base, "slab", to_owner)

    base, bulk_in = lax.optimization_barrier((base, bulk_in))
    mask_in = bulk_in[FIXED * tile : FIXED * tile + n_tile, :n_tile].astype(jnp.int32)
    sizes = (0, slots - FIXED)

    def send(k):
        def branch(tiles):
            if k == 0:
                return jnp.zeros_like(tiles)
            return lax.ppermute(tiles, "slab", to_owner)

        return branch

    over = jnp.sum(jnp.where(owner, mask_in, slab_mask)) - FIXED
    which = sum((over > k).astype(jnp.int32) for k in sizes[:-1])
    extra_in = lax.switch(which, [send(k) for k in sizes], extra)

    pair, back = local_call(
        functools.partial(pair_kernel, tile),
        (slab_mask, mask_in, slab_tiles, bulk_in, extra_in, vectors),
        (square, block),
    )
    back_in = lax.ppermute(back, "slab", from_owner)
    first_own, back2 = local_call(first_kernel, (base, pair, vecs_in), (block, block))
    back2_in = lax.ppermute(back2, "slab", from_owner)

    far = local_call(far_kernel, (pair, base_in, back), block)
    first = jnp.where(owner, first_own, (base + back_in) / HALF_SPAN)
    first_grp = [lax.ppermute(x, "grp", grp_pairs) for x in jnp.split(first, 2, axis=0)]
    near = local_call(near_kernel, (sym, across, first, *first_grp), block)
    total = near + jnp.where(owner, far, back2_in)
    return 2.0 * total / HALF_SPAN - vectors


def solution(mesh):
    spec = P(("grp", "slab"), None)
    return jax.shard_map(body, mesh=mesh, in_specs=(spec,) * 6, out_specs=spec, check_vma=False)
```

```python
import functools

import jax
import jax.numpy as jnp
from jax import lax
from jax.experimental import pallas as pl
from jax.experimental.pallas import tpu as pltpu
from jax.sharding import PartitionSpec as P

CENTER = 0.5
HALF_SPAN = 5.0
SIZES = (4, 5, 6, 7, 8, 9, 10, 12, 16)
COST = 1000
GRP_CUTS = 2


def split(x):
    high = x.astype(jnp.bfloat16)
    return high, (x - high.astype(jnp.float32)).astype(jnp.bfloat16)


def product(a, b):
    dot = functools.partial(jnp.dot, preferred_element_type=jnp.float32)
    return dot(a[0], b[0]) + (dot(a[0], b[1]) + dot(a[1], b[0]))


def owns(slab, half):
    return (slab < half) == (slab % 2 == 0)


def pack_kernel(tile, slab_mask, slab_ref, out_ref):
    n = slab_ref.shape[0] // tile
    out_ref[...] = jnp.zeros_like(out_ref)
    slot = jnp.int32(0)
    for i in range(n):
        for j in range(n):
            stored = slab_mask[i, j] > 0

            @pl.when(stored)
            def _():
                out_ref[slot] = slab_ref[i * tile : (i + 1) * tile, j * tile : (j + 1) * tile]

            slot = slot + stored.astype(jnp.int32)


def masked_kernel(tile, mask, tiles_ref, *out_refs):
    n = tiles_ref.shape[0] // tile
    for i in range(n):
        out_ref = out_refs[i * len(out_refs) // n]
        top = i * tile % out_ref.shape[0]
        for j in range(n):
            cols = slice(j * tile, (j + 1) * tile)
            out_ref[top : top + tile, cols] = tiles_ref[i * tile : (i + 1) * tile, cols] * mask[i, j].astype(jnp.float32)


def pair_kernel(tile, own_mask, in_mask, own_ref, slots_ref, vec_ref, out_ref, back_ref):
    n = own_ref.shape[0] // tile
    slot = jnp.int32(0)
    for i in range(n):
        for j in range(n):
            at = (slice(i * tile, (i + 1) * tile), slice(j * tile, (j + 1) * tile))
            out_ref[at] = own_ref[at] * own_mask[i, j].astype(jnp.float32)
    for i in range(n):
        for j in range(n):
            to = (slice(j * tile, (j + 1) * tile), slice(i * tile, (i + 1) * tile))
            stored = in_mask[i, j] > 0

            @pl.when(stored)
            def _():
                out_ref[to] += slots_ref[slot].T

            slot = slot + stored.astype(jnp.int32)
    back_ref[...] = product(split(out_ref[...].T), split(vec_ref[...]))


def base_kernel(vec_ref, diag_ref, vec_grp_ref, *refs):
    *grp_refs, base_ref, sym_ref, across_ref = refs
    half = len(grp_refs) // 2
    grp, grp_in = (jnp.concatenate([ref[...] for ref in part], axis=0) for part in (grp_refs[:half], grp_refs[half:]))
    raw = diag_ref[...]
    row = lax.broadcasted_iota(jnp.int32, raw.shape, 0)
    col = lax.broadcasted_iota(jnp.int32, raw.shape, 1)
    sym = 0.5 * (raw + raw.T) - jnp.where(row == col, jnp.float32(CENTER), jnp.float32(0))
    across = grp + grp_in.T
    sym_ref[...] = sym
    across_ref[...] = across
    base_ref[...] = product(split(sym), split(vec_ref[...])) + product(split(across), split(vec_grp_ref[...]))


def first_kernel(base_ref, pair_ref, vec_in_ref, first_ref, back_ref):
    pair = pair_ref[...]
    first = (base_ref[...] + product(split(pair), split(vec_in_ref[...]))) / HALF_SPAN
    first_ref[...] = first
    back_ref[...] = product(split(pair.T), split(first))


def near_kernel(sym_ref, across_ref, first_ref, *refs):
    *first_grp_refs, near_ref = refs
    first_grp = jnp.concatenate([ref[...] for ref in first_grp_refs], axis=0)
    near_ref[...] = product(split(sym_ref[...]), split(first_ref[...])) + product(
        split(across_ref[...]), split(first_grp)
    )


def far_kernel(pair_ref, base_in_ref, back_ref, far_ref):
    first = (base_in_ref[...] + back_ref[...]) / HALF_SPAN
    far_ref[...] = product(split(pair_ref[...]), split(first))


def local_call(kernel, ins, out_shape):
    spaces = [pl.BlockSpec(memory_space=pltpu.SMEM if x.dtype == jnp.int32 else pltpu.VMEM) for x in ins]
    many = isinstance(out_shape, tuple)
    vmem = pl.BlockSpec(memory_space=pltpu.VMEM)
    return pl.pallas_call(
        kernel,
        out_shape=out_shape,
        in_specs=spaces,
        out_specs=(vmem,) * len(out_shape) if many else vmem,
        compiler_params=pltpu.CompilerParams(vmem_limit_bytes=24 * 1024 * 1024),
        cost_estimate=pl.CostEstimate(flops=COST, bytes_accessed=COST, transcendentals=0),
    )(*ins)


def body(vectors, diag_block, slab_tiles, slab_mask, grp_tiles, grp_mask):
    rows, n_tile = slab_tiles.shape[0], slab_mask.shape[0]
    tile = rows // n_tile
    slots = n_tile * n_tile
    n_slab, n_grp = lax.axis_size("slab"), lax.axis_size("grp")
    half = n_slab // 2
    owner = owns(lax.axis_index("slab"), half)
    to_owner = [(i, i ^ half) for i in range(n_slab) if not owns(i, half)]
    from_owner = [(i, i ^ half) for i in range(n_slab) if owns(i, half)]
    grp_pairs = [(i, i ^ (n_grp // 2)) for i in range(n_grp)]
    f32 = jnp.float32
    square = jax.ShapeDtypeStruct((rows, rows), f32)
    block = jax.ShapeDtypeStruct(vectors.shape, f32)

    mask_in = lax.ppermute(slab_mask, "slab", to_owner)
    vecs_in = lax.ppermute(vectors, "slab", to_owner)
    packed = local_call(
        functools.partial(pack_kernel, tile),
        (slab_mask, slab_tiles),
        jax.ShapeDtypeStruct((slots, tile, tile), f32),
    )
    later = vectors
    vecs_grp = lax.ppermute(later, "grp", grp_pairs)

    grp_blocks = local_call(
        functools.partial(masked_kernel, tile),
        (grp_mask, grp_tiles),
        (jax.ShapeDtypeStruct((rows // GRP_CUTS, rows), f32),) * GRP_CUTS,
    )
    grp_in = [lax.ppermute(x, "grp", grp_pairs) for x in grp_blocks]

    base, sym, across = local_call(
        base_kernel, (vectors, diag_block, vecs_grp, *grp_blocks, *grp_in), (block, square, square)
    )
    base_in = lax.ppermute(base, "slab", to_owner)

    def send(k):
        def branch(tiles, own_mask, in_mask, own, vecs):
            got = lax.ppermute(tiles[:k], "slab", to_owner)
            return local_call(
                functools.partial(pair_kernel, tile), (own_mask, in_mask, own, got, vecs), (square, block)
            )

        return branch

    count = jnp.sum(jnp.where(owner, mask_in, slab_mask))
    which = sum((count > k).astype(jnp.int32) for k in SIZES[:-1])
    pair, back = lax.switch(which, [send(k) for k in SIZES], packed, slab_mask, mask_in, slab_tiles, vectors)
    back_in = lax.ppermute(back, "slab", from_owner)
    first_own, back2 = local_call(first_kernel, (base, pair, vecs_in), (block, block))
    back2_in = lax.ppermute(back2, "slab", from_owner)

    far = local_call(far_kernel, (pair, base_in, back), block)
    first = jnp.where(owner, first_own, (base + back_in) / HALF_SPAN)
    first_grp = [lax.ppermute(x, "grp", grp_pairs) for x in jnp.split(first, 2, axis=0)]
    near = local_call(near_kernel, (sym, across, first, *first_grp), block)
    total = near + jnp.where(owner, far, back2_in)
    return 2.0 * total / HALF_SPAN - vectors


def solution(mesh):
    spec = P(("grp", "slab"), None)
    return jax.shard_map(body, mesh=mesh, in_specs=(spec,) * 6, out_specs=spec, check_vma=False)
```

```python
import functools

import jax
import jax.numpy as jnp
from jax import lax
from jax.experimental import pallas as pl
from jax.experimental.pallas import tpu as pltpu
from jax.sharding import PartitionSpec as P

CENTER = 0.5
HALF_SPAN = 5.0
FIXED = 12
COST = 1000
GRP_CUTS = 2


def split(x):
    high = x.astype(jnp.bfloat16)
    return high, (x - high.astype(jnp.float32)).astype(jnp.bfloat16)


def product(a, b):
    dot = functools.partial(jnp.dot, preferred_element_type=jnp.float32)
    return dot(a[0], b[0]) + (dot(a[0], b[1]) + dot(a[1], b[0]))


def owns(slab, half):
    return (slab < half) == (slab % 2 == 0)


def pack_kernel(tile, slab_mask, slab_ref, bulk_ref, extra_ref):
    n = slab_ref.shape[0] // tile
    bulk_ref[...] = jnp.zeros_like(bulk_ref)
    extra_ref[...] = jnp.zeros_like(extra_ref)
    tail = (bulk_ref.shape[0] - FIXED * tile, tile)
    row, col = lax.broadcasted_iota(jnp.int32, tail, 0), lax.broadcasted_iota(jnp.int32, tail, 1)
    mask = jnp.zeros(tail, jnp.float32)
    slot = jnp.int32(0)
    for i in range(n):
        for j in range(n):
            at = (slice(i * tile, (i + 1) * tile), slice(j * tile, (j + 1) * tile))
            stored = slab_mask[i, j] > 0
            mask = jnp.where(jnp.logical_and(row == i, col == j), slab_mask[i, j].astype(jnp.float32), mask)

            @pl.when(jnp.logical_and(stored, slot < FIXED))
            def _():
                bulk_ref[pl.ds(pl.multiple_of(slot * tile, tile), tile), :] = slab_ref[at]

            @pl.when(jnp.logical_and(stored, slot >= FIXED))
            def _():
                extra_ref[slot - FIXED] = slab_ref[at]

            slot = slot + stored.astype(jnp.int32)
    bulk_ref[FIXED * tile :, :] = mask


def masked_kernel(tile, mask, tiles_ref, *out_refs):
    n = tiles_ref.shape[0] // tile
    for i in range(n):
        out_ref = out_refs[i * len(out_refs) // n]
        top = i * tile % out_ref.shape[0]
        for j in range(n):
            cols = slice(j * tile, (j + 1) * tile)
            out_ref[top : top + tile, cols] = tiles_ref[i * tile : (i + 1) * tile, cols] * mask[i, j].astype(jnp.float32)


def pair_kernel(tile, own_mask, in_mask, own_ref, bulk_ref, extra_ref, vec_ref, out_ref, back_ref):
    n = own_ref.shape[0] // tile
    for i in range(n):
        for j in range(n):
            at = (slice(i * tile, (i + 1) * tile), slice(j * tile, (j + 1) * tile))
            out_ref[at] = own_ref[at] * own_mask[i, j].astype(jnp.float32)
    slot = jnp.int32(0)
    for i in range(n):
        for j in range(n):
            to = (slice(j * tile, (j + 1) * tile), slice(i * tile, (i + 1) * tile))
            stored = in_mask[i, j] > 0

            @pl.when(jnp.logical_and(stored, slot < FIXED))
            def _():
                out_ref[to] += bulk_ref[pl.ds(pl.multiple_of(slot * tile, tile), tile), :].T

            @pl.when(jnp.logical_and(stored, slot >= FIXED))
            def _():
                out_ref[to] += extra_ref[slot - FIXED].T

            slot = slot + stored.astype(jnp.int32)
    back_ref[...] = product(split(out_ref[...].T), split(vec_ref[...]))


def base_kernel(vec_ref, diag_ref, vec_grp_ref, *refs):
    *grp_refs, base_ref, sym_ref, across_ref = refs
    half = len(grp_refs) // 2
    grp, grp_in = (jnp.concatenate([ref[...] for ref in part], axis=0) for part in (grp_refs[:half], grp_refs[half:]))
    raw = diag_ref[...]
    row = lax.broadcasted_iota(jnp.int32, raw.shape, 0)
    col = lax.broadcasted_iota(jnp.int32, raw.shape, 1)
    sym = 0.5 * (raw + raw.T) - jnp.where(row == col, jnp.float32(CENTER), jnp.float32(0))
    across = grp + grp_in.T
    sym_ref[...] = sym
    across_ref[...] = across
    base_ref[...] = product(split(sym), split(vec_ref[...])) + product(split(across), split(vec_grp_ref[...]))


def first_kernel(base_ref, pair_ref, vec_in_ref, first_ref, back_ref):
    pair = pair_ref[...]
    first = (base_ref[...] + product(split(pair), split(vec_in_ref[...]))) / HALF_SPAN
    first_ref[...] = first
    back_ref[...] = product(split(pair.T), split(first))


def near_kernel(sym_ref, across_ref, first_ref, *refs):
    *first_grp_refs, near_ref = refs
    first_grp = jnp.concatenate([ref[...] for ref in first_grp_refs], axis=0)
    near_ref[...] = product(split(sym_ref[...]), split(first_ref[...])) + product(
        split(across_ref[...]), split(first_grp)
    )


def far_kernel(pair_ref, base_in_ref, back_ref, far_ref):
    first = (base_in_ref[...] + back_ref[...]) / HALF_SPAN
    far_ref[...] = product(split(pair_ref[...]), split(first))


def local_call(kernel, ins, out_shape):
    spaces = [pl.BlockSpec(memory_space=pltpu.SMEM if x.dtype == jnp.int32 else pltpu.VMEM) for x in ins]
    many = isinstance(out_shape, tuple)
    vmem = pl.BlockSpec(memory_space=pltpu.VMEM)
    return pl.pallas_call(
        kernel,
        out_shape=out_shape,
        in_specs=spaces,
        out_specs=(vmem,) * len(out_shape) if many else vmem,
        compiler_params=pltpu.CompilerParams(vmem_limit_bytes=24 * 1024 * 1024),
        cost_estimate=pl.CostEstimate(flops=COST, bytes_accessed=COST, transcendentals=0),
    )(*ins)


def body(vectors, diag_block, slab_tiles, slab_mask, grp_tiles, grp_mask):
    rows, n_tile = slab_tiles.shape[0], slab_mask.shape[0]
    tile = rows // n_tile
    slots = n_tile * n_tile
    n_slab, n_grp = lax.axis_size("slab"), lax.axis_size("grp")
    half = n_slab // 2
    owner = owns(lax.axis_index("slab"), half)
    to_owner = [(i, i ^ half) for i in range(n_slab) if not owns(i, half)]
    from_owner = [(i, i ^ half) for i in range(n_slab) if owns(i, half)]
    grp_pairs = [(i, i ^ (n_grp // 2)) for i in range(n_grp)]
    f32 = jnp.float32
    square = jax.ShapeDtypeStruct((rows, rows), f32)
    block = jax.ShapeDtypeStruct(vectors.shape, f32)

    vecs_grp = lax.ppermute(vectors, "grp", grp_pairs)
    vecs_in = lax.ppermute(vectors, "slab", to_owner)

    bulk, extra = local_call(
        functools.partial(pack_kernel, tile),
        (slab_mask, slab_tiles),
        (
            jax.ShapeDtypeStruct((FIXED * tile + 8, tile), f32),
            jax.ShapeDtypeStruct((slots - FIXED, tile, tile), f32),
        ),
    )
    bulk_in = lax.ppermute(bulk, "slab", to_owner)
    grp_blocks = local_call(
        functools.partial(masked_kernel, tile),
        (grp_mask, grp_tiles),
        (jax.ShapeDtypeStruct((rows // GRP_CUTS, rows), f32),) * GRP_CUTS,
    )
    grp_in = [lax.ppermute(x, "grp", grp_pairs) for x in grp_blocks]

    base, sym, across = local_call(
        base_kernel, (vectors, diag_block, vecs_grp, *grp_blocks, *grp_in), (block, square, square)
    )
    base_in = lax.ppermute(base, "slab", to_owner)

    base, bulk_in = lax.optimization_barrier((base, bulk_in))
    mask_in = bulk_in[FIXED * tile : FIXED * tile + n_tile, :n_tile].astype(jnp.int32)
    sizes = (0, slots - FIXED)

    def send(k):
        def branch(tiles):
            if k == 0:
                return jnp.zeros_like(tiles)
            return lax.ppermute(tiles, "slab", to_owner)

        return branch

    over = jnp.sum(jnp.where(owner, mask_in, slab_mask)) - FIXED
    which = sum((over > k).astype(jnp.int32) for k in sizes[:-1])
    extra_in = lax.switch(which, [send(k) for k in sizes], extra)

    pair, back = local_call(
        functools.partial(pair_kernel, tile),
        (slab_mask, mask_in, slab_tiles, bulk_in, extra_in, vectors),
        (square, block),
    )
    back_in = lax.ppermute(back, "slab", from_owner)
    first_own, back2 = local_call(first_kernel, (base, pair, vecs_in), (block, block))
    back2, back_in = lax.optimization_barrier((back2, back_in))
    back2_in = lax.ppermute(back2, "slab", from_owner)

    far = local_call(far_kernel, (pair, base_in, back), block)
    first = jnp.where(owner, first_own, (base + back_in) / HALF_SPAN)
    first_grp = [lax.ppermute(x, "grp", grp_pairs) for x in jnp.split(first, 2, axis=0)]
    near = local_call(near_kernel, (sym, across, first, *first_grp), block)
    total = near + jnp.where(owner, far, back2_in)
    return 2.0 * total / HALF_SPAN - vectors


def solution(mesh):
    spec = P(("grp", "slab"), None)
    return jax.shard_map(body, mesh=mesh, in_specs=(spec,) * 6, out_specs=spec, check_vma=False)
```

```python
import functools

import jax
import jax.numpy as jnp
from jax import lax
from jax.experimental import pallas as pl
from jax.experimental.pallas import tpu as pltpu
from jax.sharding import PartitionSpec as P

CENTER = 0.5
HALF_SPAN = 5.0
FIXED = 12
COST = 1000
GRP_CUTS = 2
CUTS = 2


def split(x):
    high = x.astype(jnp.bfloat16)
    return high, (x - high.astype(jnp.float32)).astype(jnp.bfloat16)


def product(a, b):
    dot = functools.partial(jnp.dot, preferred_element_type=jnp.float32)
    return dot(a[0], b[0]) + (dot(a[0], b[1]) + dot(a[1], b[0]))


def owns(slab, half):
    return (slab < half) == (slab % 2 == 0)


def pack_kernel(tile, slab_mask, slab_ref, bulk_ref, extra_ref):
    n = slab_ref.shape[0] // tile
    bulk_ref[...] = jnp.zeros_like(bulk_ref)
    extra_ref[...] = jnp.zeros_like(extra_ref)
    tail = (bulk_ref.shape[0] - FIXED * tile, tile)
    row, col = lax.broadcasted_iota(jnp.int32, tail, 0), lax.broadcasted_iota(jnp.int32, tail, 1)
    mask = jnp.zeros(tail, jnp.float32)
    slot = jnp.int32(0)
    for i in range(n):
        for j in range(n):
            at = (slice(i * tile, (i + 1) * tile), slice(j * tile, (j + 1) * tile))
            stored = slab_mask[i, j] > 0
            mask = jnp.where(jnp.logical_and(row == i, col == j), slab_mask[i, j].astype(jnp.float32), mask)

            @pl.when(jnp.logical_and(stored, slot < FIXED))
            def _():
                bulk_ref[pl.ds(pl.multiple_of(slot * tile, tile), tile), :] = slab_ref[at]

            @pl.when(jnp.logical_and(stored, slot >= FIXED))
            def _():
                extra_ref[slot - FIXED] = slab_ref[at]

            slot = slot + stored.astype(jnp.int32)
    bulk_ref[FIXED * tile :, :] = mask


def masked_kernel(tile, mask, tiles_ref, *out_refs):
    n = tiles_ref.shape[0] // tile
    for i in range(n):
        out_ref = out_refs[i * len(out_refs) // n]
        top = i * tile % out_ref.shape[0]
        for j in range(n):
            cols = slice(j * tile, (j + 1) * tile)
            out_ref[top : top + tile, cols] = tiles_ref[i * tile : (i + 1) * tile, cols] * mask[i, j].astype(jnp.float32)


def pair_kernel(tile, own_mask, in_mask, own_ref, bulk_ref, extra_ref, vec_ref, out_ref, *back_refs):
    n = own_ref.shape[0] // tile
    for i in range(n):
        for j in range(n):
            at = (slice(i * tile, (i + 1) * tile), slice(j * tile, (j + 1) * tile))
            out_ref[at] = own_ref[at] * own_mask[i, j].astype(jnp.float32)
    slot = jnp.int32(0)
    for i in range(n):
        for j in range(n):
            to = (slice(j * tile, (j + 1) * tile), slice(i * tile, (i + 1) * tile))
            stored = in_mask[i, j] > 0

            @pl.when(jnp.logical_and(stored, slot < FIXED))
            def _():
                out_ref[to] += bulk_ref[pl.ds(pl.multiple_of(slot * tile, tile), tile), :].T

            @pl.when(jnp.logical_and(stored, slot >= FIXED))
            def _():
                out_ref[to] += extra_ref[slot - FIXED].T

            slot = slot + stored.astype(jnp.int32)
    back, top = product(split(out_ref[...].T), split(vec_ref[...])), 0
    for ref in back_refs:
        ref[...] = back[top : top + ref.shape[0]]
        top += ref.shape[0]


def base_kernel(vec_ref, diag_ref, vec_grp_ref, *refs):
    *grp_refs, base_ref, sym_ref, across_ref = refs
    half = len(grp_refs) // 2
    grp, grp_in = (jnp.concatenate([ref[...] for ref in part], axis=0) for part in (grp_refs[:half], grp_refs[half:]))
    raw = diag_ref[...]
    row = lax.broadcasted_iota(jnp.int32, raw.shape, 0)
    col = lax.broadcasted_iota(jnp.int32, raw.shape, 1)
    sym = 0.5 * (raw + raw.T) - jnp.where(row == col, jnp.float32(CENTER), jnp.float32(0))
    across = grp + grp_in.T
    sym_ref[...] = sym
    across_ref[...] = across
    base_ref[...] = product(split(sym), split(vec_ref[...])) + product(split(across), split(vec_grp_ref[...]))


def first_kernel(base_ref, pair_ref, vec_in_ref, first_ref, back_ref):
    pair = pair_ref[...]
    first = (base_ref[...] + product(split(pair), split(vec_in_ref[...]))) / HALF_SPAN
    first_ref[...] = first
    back_ref[...] = product(split(pair.T), split(first))


def step_kernel(top, owner, own_ref, base_ref, back_ref, out_ref):
    rows = slice(top, top + out_ref.shape[0])
    stepped = (base_ref[rows] + back_ref[...]) / HALF_SPAN
    out_ref[...] = jnp.where(owner[0, 0] > 0, own_ref[rows], stepped)


def near_kernel(sym_ref, across_ref, *refs):
    *first_refs, near_ref = refs
    half = len(first_refs) // 2
    first, first_grp = (
        jnp.concatenate([ref[...] for ref in part], axis=0) for part in (first_refs[:half], first_refs[half:])
    )
    near_ref[...] = product(split(sym_ref[...]), split(first)) + product(split(across_ref[...]), split(first_grp))


def far_kernel(pair_ref, base_in_ref, *refs):
    *back_refs, far_ref = refs
    first = (base_in_ref[...] + jnp.concatenate([ref[...] for ref in back_refs], axis=0)) / HALF_SPAN
    far_ref[...] = product(split(pair_ref[...]), split(first))


def local_call(kernel, ins, out_shape):
    spaces = [pl.BlockSpec(memory_space=pltpu.SMEM if x.dtype == jnp.int32 else pltpu.VMEM) for x in ins]
    many = isinstance(out_shape, tuple)
    vmem = pl.BlockSpec(memory_space=pltpu.VMEM)
    return pl.pallas_call(
        kernel,
        out_shape=out_shape,
        in_specs=spaces,
        out_specs=(vmem,) * len(out_shape) if many else vmem,
        compiler_params=pltpu.CompilerParams(vmem_limit_bytes=24 * 1024 * 1024),
        cost_estimate=pl.CostEstimate(flops=COST, bytes_accessed=COST, transcendentals=0),
    )(*ins)


def body(vectors, diag_block, slab_tiles, slab_mask, grp_tiles, grp_mask):
    rows, n_tile = slab_tiles.shape[0], slab_mask.shape[0]
    tile = rows // n_tile
    slots = n_tile * n_tile
    n_slab, n_grp = lax.axis_size("slab"), lax.axis_size("grp")
    half = n_slab // 2
    owner = owns(lax.axis_index("slab"), half)
    to_owner = [(i, i ^ half) for i in range(n_slab) if not owns(i, half)]
    from_owner = [(i, i ^ half) for i in range(n_slab) if owns(i, half)]
    grp_pairs = [(i, i ^ (n_grp // 2)) for i in range(n_grp)]
    f32 = jnp.float32
    square = jax.ShapeDtypeStruct((rows, rows), f32)
    block = jax.ShapeDtypeStruct(vectors.shape, f32)

    vecs_grp = lax.ppermute(vectors, "grp", grp_pairs)
    vecs_in = lax.ppermute(vectors, "slab", to_owner)

    bulk, extra = local_call(
        functools.partial(pack_kernel, tile),
        (slab_mask, slab_tiles),
        (
            jax.ShapeDtypeStruct((FIXED * tile + 8, tile), f32),
            jax.ShapeDtypeStruct((slots - FIXED, tile, tile), f32),
        ),
    )
    bulk_in = lax.ppermute(bulk, "slab", to_owner)
    grp_blocks = local_call(
        functools.partial(masked_kernel, tile),
        (grp_mask, grp_tiles),
        (jax.ShapeDtypeStruct((rows // GRP_CUTS, rows), f32),) * GRP_CUTS,
    )
    grp_in = [lax.ppermute(x, "grp", grp_pairs) for x in grp_blocks]

    base, sym, across = local_call(
        base_kernel, (vectors, diag_block, vecs_grp, *grp_blocks, *grp_in), (block, square, square)
    )
    base_in = lax.ppermute(base, "slab", to_owner)

    base, bulk_in = lax.optimization_barrier((base, bulk_in))
    mask_in = bulk_in[FIXED * tile : FIXED * tile + n_tile, :n_tile].astype(jnp.int32)
    sizes = (0, slots - FIXED)

    def send(k):
        def branch(tiles):
            if k == 0:
                return jnp.zeros_like(tiles)
            return lax.ppermute(tiles, "slab", to_owner)

        return branch

    over = jnp.sum(jnp.where(owner, mask_in, slab_mask)) - FIXED
    which = sum((over > k).astype(jnp.int32) for k in sizes[:-1])
    extra_in = lax.switch(which, [send(k) for k in sizes], extra)

    half_block = jax.ShapeDtypeStruct((rows // CUTS, vectors.shape[1]), f32)
    pair, *back = local_call(
        functools.partial(pair_kernel, tile),
        (slab_mask, mask_in, slab_tiles, bulk_in, extra_in, vectors),
        (square,) + (half_block,) * CUTS,
    )
    back_in = [lax.ppermute(x, "slab", from_owner) for x in back]
    first_own, back2 = local_call(first_kernel, (base, pair, vecs_in), (block, block))
    back2, back_in[0] = lax.optimization_barrier((back2, back_in[0]))
    back2_in = lax.ppermute(back2, "slab", from_owner)

    far = local_call(far_kernel, (pair, base_in, *back), block)
    role = owner.astype(jnp.int32).reshape(1, 1)
    first = [
        local_call(
            functools.partial(step_kernel, at * half_block.shape[0]), (role, first_own, base, got), half_block
        )
        for at, got in enumerate(back_in)
    ]
    first_grp = [lax.ppermute(x, "grp", grp_pairs) for x in first]
    near = local_call(near_kernel, (sym, across, *first, *first_grp), block)
    total = near + jnp.where(owner, far, back2_in)
    return 2.0 * total / HALF_SPAN - vectors


def solution(mesh):
    spec = P(("grp", "slab"), None)
    return jax.shard_map(body, mesh=mesh, in_specs=(spec,) * 6, out_specs=spec, check_vma=False)
```

```python
import functools

import jax
import jax.numpy as jnp
from jax import lax
from jax.experimental import pallas as pl
from jax.experimental.pallas import tpu as pltpu
from jax.sharding import PartitionSpec as P

CENTER = 0.5
HALF_SPAN = 5.0
FIXED = 12
COST = 1000
GRP_CUTS = 2


def split(x):
    high = x.astype(jnp.bfloat16)
    return high, (x - high.astype(jnp.float32)).astype(jnp.bfloat16)


def product(a, b):
    dot = functools.partial(jnp.dot, preferred_element_type=jnp.float32)
    return dot(a[0], b[0]) + (dot(a[0], b[1]) + dot(a[1], b[0]))


def owns(slab, half):
    return (slab < half) == (slab % 2 == 0)


def pack_kernel(tile, slab_mask, slab_ref, bulk_ref, extra_ref):
    n = slab_ref.shape[0] // tile
    bulk_ref[...] = jnp.zeros_like(bulk_ref)
    extra_ref[...] = jnp.zeros_like(extra_ref)
    tail = (bulk_ref.shape[0] - FIXED * tile, tile)
    row, col = lax.broadcasted_iota(jnp.int32, tail, 0), lax.broadcasted_iota(jnp.int32, tail, 1)
    mask = jnp.zeros(tail, jnp.float32)
    slot = jnp.int32(0)
    for i in range(n):
        for j in range(n):
            at = (slice(i * tile, (i + 1) * tile), slice(j * tile, (j + 1) * tile))
            stored = slab_mask[i, j] > 0
            mask = jnp.where(jnp.logical_and(row == i, col == j), slab_mask[i, j].astype(jnp.float32), mask)

            @pl.when(jnp.logical_and(stored, slot < FIXED))
            def _():
                bulk_ref[pl.ds(pl.multiple_of(slot * tile, tile), tile), :] = slab_ref[at]

            @pl.when(jnp.logical_and(stored, slot >= FIXED))
            def _():
                extra_ref[slot - FIXED] = slab_ref[at]

            slot = slot + stored.astype(jnp.int32)
    bulk_ref[FIXED * tile :, :] = mask


def masked_kernel(tile, mask, tiles_ref, *out_refs):
    n = tiles_ref.shape[0] // tile
    for i in range(n):
        out_ref = out_refs[i * len(out_refs) // n]
        top = i * tile % out_ref.shape[0]
        for j in range(n):
            cols = slice(j * tile, (j + 1) * tile)
            out_ref[top : top + tile, cols] = tiles_ref[i * tile : (i + 1) * tile, cols] * mask[i, j].astype(jnp.float32)


def pair_kernel(tile, own_mask, in_mask, own_ref, bulk_ref, extra_ref, vec_ref, out_ref, back_ref):
    n = own_ref.shape[0] // tile
    for i in range(n):
        for j in range(n):
            at = (slice(i * tile, (i + 1) * tile), slice(j * tile, (j + 1) * tile))
            out_ref[at] = own_ref[at] * own_mask[i, j].astype(jnp.float32)
    slot = jnp.int32(0)
    for i in range(n):
        for j in range(n):
            to = (slice(j * tile, (j + 1) * tile), slice(i * tile, (i + 1) * tile))
            stored = in_mask[i, j] > 0

            @pl.when(jnp.logical_and(stored, slot < FIXED))
            def _():
                out_ref[to] += bulk_ref[pl.ds(pl.multiple_of(slot * tile, tile), tile), :].T

            @pl.when(jnp.logical_and(stored, slot >= FIXED))
            def _():
                out_ref[to] += extra_ref[slot - FIXED].T

            slot = slot + stored.astype(jnp.int32)
    back_ref[...] = product(split(out_ref[...].T), split(vec_ref[...]))


def base_kernel(vec_ref, diag_ref, vec_grp_ref, *refs):
    *grp_refs, base_ref, sym_ref, across_ref = refs
    half = len(grp_refs) // 2
    grp, grp_in = (jnp.concatenate([ref[...] for ref in part], axis=0) for part in (grp_refs[:half], grp_refs[half:]))
    raw = diag_ref[...]
    row = lax.broadcasted_iota(jnp.int32, raw.shape, 0)
    col = lax.broadcasted_iota(jnp.int32, raw.shape, 1)
    sym = 0.5 * (raw + raw.T) - jnp.where(row == col, jnp.float32(CENTER), jnp.float32(0))
    across = grp + grp_in.T
    sym_ref[...] = sym
    across_ref[...] = across
    base_ref[...] = product(split(sym), split(vec_ref[...])) + product(split(across), split(vec_grp_ref[...]))


def first_kernel(base_ref, pair_ref, vec_in_ref, base_in_ref, back_ref, first_ref, back2_ref, far_ref):
    pair = split(pair_ref[...])
    first = (base_ref[...] + product(pair, split(vec_in_ref[...]))) / HALF_SPAN
    first_ref[...] = first
    back2_ref[...] = product(split(pair_ref[...].T), split(first))
    far_ref[...] = product(pair, split((base_in_ref[...] + back_ref[...]) / HALF_SPAN))


def near_kernel(sym_ref, across_ref, first_ref, *refs):
    *first_grp_refs, near_ref = refs
    first_grp = jnp.concatenate([ref[...] for ref in first_grp_refs], axis=0)
    near_ref[...] = product(split(sym_ref[...]), split(first_ref[...])) + product(
        split(across_ref[...]), split(first_grp)
    )


def local_call(kernel, ins, out_shape):
    spaces = [pl.BlockSpec(memory_space=pltpu.SMEM if x.dtype == jnp.int32 else pltpu.VMEM) for x in ins]
    many = isinstance(out_shape, tuple)
    vmem = pl.BlockSpec(memory_space=pltpu.VMEM)
    return pl.pallas_call(
        kernel,
        out_shape=out_shape,
        in_specs=spaces,
        out_specs=(vmem,) * len(out_shape) if many else vmem,
        compiler_params=pltpu.CompilerParams(vmem_limit_bytes=24 * 1024 * 1024),
        cost_estimate=pl.CostEstimate(flops=COST, bytes_accessed=COST, transcendentals=0),
    )(*ins)


def body(vectors, diag_block, slab_tiles, slab_mask, grp_tiles, grp_mask):
    rows, n_tile = slab_tiles.shape[0], slab_mask.shape[0]
    tile = rows // n_tile
    slots = n_tile * n_tile
    n_slab, n_grp = lax.axis_size("slab"), lax.axis_size("grp")
    half = n_slab // 2
    owner = owns(lax.axis_index("slab"), half)
    to_owner = [(i, i ^ half) for i in range(n_slab) if not owns(i, half)]
    from_owner = [(i, i ^ half) for i in range(n_slab) if owns(i, half)]
    grp_pairs = [(i, i ^ (n_grp // 2)) for i in range(n_grp)]
    f32 = jnp.float32
    square = jax.ShapeDtypeStruct((rows, rows), f32)
    block = jax.ShapeDtypeStruct(vectors.shape, f32)

    vecs_grp = lax.ppermute(vectors, "grp", grp_pairs)
    vecs_in = lax.ppermute(vectors, "slab", to_owner)

    bulk, extra = local_call(
        functools.partial(pack_kernel, tile),
        (slab_mask, slab_tiles),
        (
            jax.ShapeDtypeStruct((FIXED * tile + 8, tile), f32),
            jax.ShapeDtypeStruct((slots - FIXED, tile, tile), f32),
        ),
    )
    bulk_in = lax.ppermute(bulk, "slab", to_owner)
    grp_blocks = local_call(
        functools.partial(masked_kernel, tile),
        (grp_mask, grp_tiles),
        (jax.ShapeDtypeStruct((rows // GRP_CUTS, rows), f32),) * GRP_CUTS,
    )
    grp_in = [lax.ppermute(x, "grp", grp_pairs) for x in grp_blocks]

    base, sym, across = local_call(
        base_kernel, (vectors, diag_block, vecs_grp, *grp_blocks, *grp_in), (block, square, square)
    )
    base_in = lax.ppermute(base, "slab", to_owner)

    base, bulk_in = lax.optimization_barrier((base, bulk_in))
    mask_in = bulk_in[FIXED * tile : FIXED * tile + n_tile, :n_tile].astype(jnp.int32)
    sizes = (0, slots - FIXED)

    def send(k):
        def branch(tiles):
            if k == 0:
                return jnp.zeros_like(tiles)
            return lax.ppermute(tiles, "slab", to_owner)

        return branch

    over = jnp.sum(jnp.where(owner, mask_in, slab_mask)) - FIXED
    which = sum((over > k).astype(jnp.int32) for k in sizes[:-1])
    extra_in = lax.switch(which, [send(k) for k in sizes], extra)

    pair, back = local_call(
        functools.partial(pair_kernel, tile),
        (slab_mask, mask_in, slab_tiles, bulk_in, extra_in, vectors),
        (square, block),
    )
    back_in = lax.ppermute(back, "slab", from_owner)
    first_own, back2, far = local_call(first_kernel, (base, pair, vecs_in, base_in, back), (block,) * 3)
    back2_in = lax.ppermute(back2, "slab", from_owner)

    first = jnp.where(owner, first_own, (base + back_in) / HALF_SPAN)
    first_grp = [lax.ppermute(x, "grp", grp_pairs) for x in jnp.split(first, 2, axis=0)]
    near = local_call(near_kernel, (sym, across, first, *first_grp), block)
    total = near + jnp.where(owner, far, back2_in)
    return 2.0 * total / HALF_SPAN - vectors


def solution(mesh):
    spec = P(("grp", "slab"), None)
    return jax.shard_map(body, mesh=mesh, in_specs=(spec,) * 6, out_specs=spec, check_vma=False)
```

```python
import functools

import jax
import jax.numpy as jnp
from jax import lax
from jax.experimental import pallas as pl
from jax.experimental.pallas import tpu as pltpu
from jax.sharding import PartitionSpec as P

CENTER = 0.5
HALF_SPAN = 5.0
FIXED = 8
COST = 1000
GRP_CUTS = 2


def split(x):
    high = x.astype(jnp.bfloat16)
    return high, (x - high.astype(jnp.float32)).astype(jnp.bfloat16)


def product(a, b):
    dot = functools.partial(jnp.dot, preferred_element_type=jnp.float32)
    return dot(a[0], b[0]) + (dot(a[0], b[1]) + dot(a[1], b[0]))


def owns(slab, half):
    return (slab < half) == (slab % 2 == 0)


def pack_kernel(tile, slab_mask, slab_ref, bulk_ref, extra_ref):
    n = slab_ref.shape[0] // tile
    bulk_ref[...] = jnp.zeros_like(bulk_ref)
    extra_ref[...] = jnp.zeros_like(extra_ref)
    slot = jnp.int32(0)
    for i in range(n):
        for j in range(n):
            at = (slice(i * tile, (i + 1) * tile), slice(j * tile, (j + 1) * tile))
            stored = slab_mask[i, j] > 0

            @pl.when(jnp.logical_and(stored, slot < FIXED))
            def _():
                bulk_ref[pl.ds(pl.multiple_of(slot * tile, tile), tile), :] = slab_ref[at]

            @pl.when(jnp.logical_and(stored, slot >= FIXED))
            def _():
                extra_ref[slot - FIXED] = slab_ref[at]

            slot = slot + stored.astype(jnp.int32)


def masked_kernel(tile, mask, tiles_ref, *out_refs):
    n = tiles_ref.shape[0] // tile
    for i in range(n):
        out_ref = out_refs[i * len(out_refs) // n]
        top = i * tile % out_ref.shape[0]
        for j in range(n):
            cols = slice(j * tile, (j + 1) * tile)
            out_ref[top : top + tile, cols] = tiles_ref[i * tile : (i + 1) * tile, cols] * mask[i, j].astype(jnp.float32)


def pair_kernel(tile, own_mask, in_mask, own_ref, bulk_ref, extra_ref, vec_ref, out_ref, back_ref):
    n = own_ref.shape[0] // tile
    for i in range(n):
        for j in range(n):
            at = (slice(i * tile, (i + 1) * tile), slice(j * tile, (j + 1) * tile))
            out_ref[at] = own_ref[at] * own_mask[i, j].astype(jnp.float32)
    slot = jnp.int32(0)
    for i in range(n):
        for j in range(n):
            to = (slice(j * tile, (j + 1) * tile), slice(i * tile, (i + 1) * tile))
            stored = in_mask[i, j] > 0

            @pl.when(jnp.logical_and(stored, slot < FIXED))
            def _():
                out_ref[to] += bulk_ref[pl.ds(pl.multiple_of(slot * tile, tile), tile), :].T

            @pl.when(jnp.logical_and(stored, slot >= FIXED))
            def _():
                out_ref[to] += extra_ref[slot - FIXED].T

            slot = slot + stored.astype(jnp.int32)
    back_ref[...] = product(split(out_ref[...].T), split(vec_ref[...]))


def base_kernel(vec_ref, diag_ref, vec_grp_ref, *refs):
    *grp_refs, base_ref, sym_ref, across_ref = refs
    half = len(grp_refs) // 2
    grp, grp_in = (jnp.concatenate([ref[...] for ref in part], axis=0) for part in (grp_refs[:half], grp_refs[half:]))
    raw = diag_ref[...]
    row = lax.broadcasted_iota(jnp.int32, raw.shape, 0)
    col = lax.broadcasted_iota(jnp.int32, raw.shape, 1)
    sym = 0.5 * (raw + raw.T) - jnp.where(row == col, jnp.float32(CENTER), jnp.float32(0))
    across = grp + grp_in.T
    sym_ref[...] = sym
    across_ref[...] = across
    base_ref[...] = product(split(sym), split(vec_ref[...])) + product(split(across), split(vec_grp_ref[...]))


def first_kernel(base_ref, pair_ref, vec_in_ref, first_ref, back_ref):
    pair = pair_ref[...]
    first = (base_ref[...] + product(split(pair), split(vec_in_ref[...]))) / HALF_SPAN
    first_ref[...] = first
    back_ref[...] = product(split(pair.T), split(first))


def near_kernel(sym_ref, across_ref, first_ref, *refs):
    *first_grp_refs, near_ref = refs
    first_grp = jnp.concatenate([ref[...] for ref in first_grp_refs], axis=0)
    near_ref[...] = product(split(sym_ref[...]), split(first_ref[...])) + product(
        split(across_ref[...]), split(first_grp)
    )


def far_kernel(pair_ref, base_in_ref, back_ref, far_ref):
    first = (base_in_ref[...] + back_ref[...]) / HALF_SPAN
    far_ref[...] = product(split(pair_ref[...]), split(first))


def local_call(kernel, ins, out_shape):
    spaces = [pl.BlockSpec(memory_space=pltpu.SMEM if x.dtype == jnp.int32 else pltpu.VMEM) for x in ins]
    many = isinstance(out_shape, tuple)
    vmem = pl.BlockSpec(memory_space=pltpu.VMEM)
    return pl.pallas_call(
        kernel,
        out_shape=out_shape,
        in_specs=spaces,
        out_specs=(vmem,) * len(out_shape) if many else vmem,
        compiler_params=pltpu.CompilerParams(vmem_limit_bytes=24 * 1024 * 1024),
        cost_estimate=pl.CostEstimate(flops=COST, bytes_accessed=COST, transcendentals=0),
    )(*ins)


def body(vectors, diag_block, slab_tiles, slab_mask, grp_tiles, grp_mask):
    rows, n_tile = slab_tiles.shape[0], slab_mask.shape[0]
    tile = rows // n_tile
    slots = n_tile * n_tile
    n_slab, n_grp = lax.axis_size("slab"), lax.axis_size("grp")
    half = n_slab // 2
    owner = owns(lax.axis_index("slab"), half)
    to_owner = [(i, i ^ half) for i in range(n_slab) if not owns(i, half)]
    from_owner = [(i, i ^ half) for i in range(n_slab) if owns(i, half)]
    grp_pairs = [(i, i ^ (n_grp // 2)) for i in range(n_grp)]
    f32 = jnp.float32
    square = jax.ShapeDtypeStruct((rows, rows), f32)
    block = jax.ShapeDtypeStruct(vectors.shape, f32)

    mask_in = lax.ppermute(slab_mask, "slab", to_owner)
    bulk, extra = local_call(
        functools.partial(pack_kernel, tile),
        (slab_mask, slab_tiles),
        (
            jax.ShapeDtypeStruct((FIXED * tile, tile), f32),
            jax.ShapeDtypeStruct((slots - FIXED, tile, tile), f32),
        ),
    )
    bulk_in = lax.ppermute(bulk, "slab", to_owner)
    sizes = (0, 2, 4, slots - FIXED)

    def send(k):
        def branch(tiles):
            if k == 0:
                return jnp.zeros_like(tiles)
            got = lax.ppermute(tiles[:k], "slab", to_owner)
            return jnp.concatenate([got, jnp.zeros((tiles.shape[0] - k, tile, tile), f32)]) if k < len(tiles) else got

        return branch

    over = jnp.sum(jnp.where(owner, mask_in, slab_mask)) - FIXED
    which = sum((over > k).astype(jnp.int32) for k in sizes[:-1])
    extra_in = lax.switch(which, [send(k) for k in sizes], extra)

    extra_in, later, later_mask = lax.optimization_barrier((extra_in, vectors, grp_mask))
    vecs_in = lax.ppermute(later, "slab", to_owner)
    vecs_grp = lax.ppermute(later, "grp", grp_pairs)
    grp_blocks = local_call(
        functools.partial(masked_kernel, tile),
        (later_mask, grp_tiles),
        (jax.ShapeDtypeStruct((rows // GRP_CUTS, rows), f32),) * GRP_CUTS,
    )
    grp_in = [lax.ppermute(x, "grp", grp_pairs) for x in grp_blocks]

    base, sym, across = local_call(
        base_kernel, (vectors, diag_block, vecs_grp, *grp_blocks, *grp_in), (block, square, square)
    )
    base_in = lax.ppermute(base, "slab", to_owner)

    pair, back = local_call(
        functools.partial(pair_kernel, tile),
        (slab_mask, mask_in, slab_tiles, bulk_in, extra_in, vectors),
        (square, block),
    )
    back_in = lax.ppermute(back, "slab", from_owner)
    first_own, back2 = local_call(first_kernel, (base, pair, vecs_in), (block, block))
    back2, back_in = lax.optimization_barrier((back2, back_in))
    back2_in = lax.ppermute(back2, "slab", from_owner)

    far = local_call(far_kernel, (pair, base_in, back), block)
    first = jnp.where(owner, first_own, (base + back_in) / HALF_SPAN)
    first_grp = [lax.ppermute(x, "grp", grp_pairs) for x in jnp.split(first, 2, axis=0)]
    near = local_call(near_kernel, (sym, across, first, *first_grp), block)
    total = near + jnp.where(owner, far, back2_in)
    return 2.0 * total / HALF_SPAN - vectors


def solution(mesh):
    spec = P(("grp", "slab"), None)
    return jax.shard_map(body, mesh=mesh, in_specs=(spec,) * 6, out_specs=spec, check_vma=False)
```

```python
import functools

import jax
import jax.numpy as jnp
from jax import lax
from jax.experimental import pallas as pl
from jax.experimental.pallas import tpu as pltpu
from jax.sharding import PartitionSpec as P

CENTER = 0.5
HALF_SPAN = 5.0
FIXED = 12
COST = 1000
GRP_CUTS = 2


def split(x):
    high = x.astype(jnp.bfloat16)
    return high, (x - high.astype(jnp.float32)).astype(jnp.bfloat16)


def product(a, b):
    dot = functools.partial(jnp.dot, preferred_element_type=jnp.float32)
    return dot(a[0], b[0]) + (dot(a[0], b[1]) + dot(a[1], b[0]))


def owns(slab, half):
    return (slab < half) == (slab % 2 == 0)


def pack_kernel(tile, slab_mask, slab_ref, bulk_ref, extra_ref):
    n = slab_ref.shape[0] // tile
    bulk_ref[...] = jnp.zeros_like(bulk_ref)
    extra_ref[...] = jnp.zeros_like(extra_ref)
    tail = (bulk_ref.shape[0] - FIXED * tile, tile)
    row, col = lax.broadcasted_iota(jnp.int32, tail, 0), lax.broadcasted_iota(jnp.int32, tail, 1)
    mask = jnp.zeros(tail, jnp.float32)
    slot = jnp.int32(0)
    for i in range(n):
        for j in range(n):
            at = (slice(i * tile, (i + 1) * tile), slice(j * tile, (j + 1) * tile))
            stored = slab_mask[i, j] > 0
            mask = jnp.where(jnp.logical_and(row == i, col == j), slab_mask[i, j].astype(jnp.float32), mask)

            @pl.when(jnp.logical_and(stored, slot < FIXED))
            def _():
                bulk_ref[pl.ds(pl.multiple_of(slot * tile, tile), tile), :] = slab_ref[at]

            @pl.when(jnp.logical_and(stored, slot >= FIXED))
            def _():
                extra_ref[slot - FIXED] = slab_ref[at]

            slot = slot + stored.astype(jnp.int32)
    bulk_ref[FIXED * tile :, :] = mask


def masked_kernel(tile, mask, tiles_ref, *out_refs):
    n = tiles_ref.shape[0] // tile
    for i in range(n):
        out_ref = out_refs[i * len(out_refs) // n]
        top = i * tile % out_ref.shape[0]
        for j in range(n):
            cols = slice(j * tile, (j + 1) * tile)
            out_ref[top : top + tile, cols] = tiles_ref[i * tile : (i + 1) * tile, cols] * mask[i, j].astype(jnp.float32)


def pair_kernel(tile, own_mask, in_mask, own_ref, bulk_ref, extra_ref, vec_ref, out_ref, back_ref):
    n = own_ref.shape[0] // tile
    for i in range(n):
        for j in range(n):
            at = (slice(i * tile, (i + 1) * tile), slice(j * tile, (j + 1) * tile))
            out_ref[at] = own_ref[at] * own_mask[i, j].astype(jnp.float32)
    slot = jnp.int32(0)
    for i in range(n):
        for j in range(n):
            to = (slice(j * tile, (j + 1) * tile), slice(i * tile, (i + 1) * tile))
            stored = in_mask[i, j] > 0

            @pl.when(jnp.logical_and(stored, slot < FIXED))
            def _():
                out_ref[to] += bulk_ref[pl.ds(pl.multiple_of(slot * tile, tile), tile), :].T

            @pl.when(jnp.logical_and(stored, slot >= FIXED))
            def _():
                out_ref[to] += extra_ref[slot - FIXED].T

            slot = slot + stored.astype(jnp.int32)
    back_ref[...] = product(split(out_ref[...].T), split(vec_ref[...]))


def base_kernel(vec_ref, diag_ref, vec_grp_ref, *refs):
    *grp_refs, base_ref, sym_ref, across_ref = refs
    half = len(grp_refs) // 2
    grp, grp_in = (jnp.concatenate([ref[...] for ref in part], axis=0) for part in (grp_refs[:half], grp_refs[half:]))
    raw = diag_ref[...]
    row = lax.broadcasted_iota(jnp.int32, raw.shape, 0)
    col = lax.broadcasted_iota(jnp.int32, raw.shape, 1)
    sym = 0.5 * (raw + raw.T) - jnp.where(row == col, jnp.float32(CENTER), jnp.float32(0))
    across = grp + grp_in.T
    sym_ref[...] = sym
    across_ref[...] = across
    base_ref[...] = product(split(sym), split(vec_ref[...])) + product(split(across), split(vec_grp_ref[...]))


def first_kernel(base_ref, pair_ref, vec_in_ref, first_ref, back_ref):
    pair = pair_ref[...]
    first = (base_ref[...] + product(split(pair), split(vec_in_ref[...]))) / HALF_SPAN
    first_ref[...] = first
    back_ref[...] = product(split(pair.T), split(first))


def near_kernel(role, sym_ref, across_ref, own_ref, own_grp_ref, other_ref, *refs):
    *other_grp_refs, near_ref = refs
    owner = role[0, 0] > 0
    other_grp = jnp.concatenate([ref[...] for ref in other_grp_refs], axis=0)
    first = jnp.where(owner, own_ref[...], other_ref[...])
    first_grp = jnp.where(owner, own_grp_ref[...], other_grp)
    near_ref[...] = product(split(sym_ref[...]), split(first)) + product(split(across_ref[...]), split(first_grp))


def far_kernel(pair_ref, base_in_ref, back_ref, far_ref):
    first = (base_in_ref[...] + back_ref[...]) / HALF_SPAN
    far_ref[...] = product(split(pair_ref[...]), split(first))


def local_call(kernel, ins, out_shape):
    spaces = [pl.BlockSpec(memory_space=pltpu.SMEM if x.dtype == jnp.int32 else pltpu.VMEM) for x in ins]
    many = isinstance(out_shape, tuple)
    vmem = pl.BlockSpec(memory_space=pltpu.VMEM)
    return pl.pallas_call(
        kernel,
        out_shape=out_shape,
        in_specs=spaces,
        out_specs=(vmem,) * len(out_shape) if many else vmem,
        compiler_params=pltpu.CompilerParams(vmem_limit_bytes=24 * 1024 * 1024),
        cost_estimate=pl.CostEstimate(flops=COST, bytes_accessed=COST, transcendentals=0),
    )(*ins)


def body(vectors, diag_block, slab_tiles, slab_mask, grp_tiles, grp_mask):
    rows, n_tile = slab_tiles.shape[0], slab_mask.shape[0]
    tile = rows // n_tile
    slots = n_tile * n_tile
    n_slab, n_grp = lax.axis_size("slab"), lax.axis_size("grp")
    half = n_slab // 2
    owner = owns(lax.axis_index("slab"), half)
    to_owner = [(i, i ^ half) for i in range(n_slab) if not owns(i, half)]
    from_owner = [(i, i ^ half) for i in range(n_slab) if owns(i, half)]
    grp_pairs = [(i, i ^ (n_grp // 2)) for i in range(n_grp)]

    def role_pairs(role):
        return [
            (g * n_slab + i, (g ^ (n_grp // 2)) * n_slab + i)
            for g in range(n_grp)
            for i in range(n_slab)
            if owns(i, half) == role
        ]

    f32 = jnp.float32
    square = jax.ShapeDtypeStruct((rows, rows), f32)
    block = jax.ShapeDtypeStruct(vectors.shape, f32)

    vecs_grp = lax.ppermute(vectors, "grp", grp_pairs)
    vecs_in = lax.ppermute(vectors, "slab", to_owner)

    bulk, extra = local_call(
        functools.partial(pack_kernel, tile),
        (slab_mask, slab_tiles),
        (
            jax.ShapeDtypeStruct((FIXED * tile + 8, tile), f32),
            jax.ShapeDtypeStruct((slots - FIXED, tile, tile), f32),
        ),
    )
    bulk_in = lax.ppermute(bulk, "slab", to_owner)
    grp_blocks = local_call(
        functools.partial(masked_kernel, tile),
        (grp_mask, grp_tiles),
        (jax.ShapeDtypeStruct((rows // GRP_CUTS, rows), f32),) * GRP_CUTS,
    )
    grp_in = [lax.ppermute(x, "grp", grp_pairs) for x in grp_blocks]

    base, sym, across = local_call(
        base_kernel, (vectors, diag_block, vecs_grp, *grp_blocks, *grp_in), (block, square, square)
    )
    base_in = lax.ppermute(base, "slab", to_owner)

    base, bulk_in = lax.optimization_barrier((base, bulk_in))
    mask_in = bulk_in[FIXED * tile : FIXED * tile + n_tile, :n_tile].astype(jnp.int32)
    sizes = (0, slots - FIXED)

    def send(k):
        def branch(tiles):
            if k == 0:
                return jnp.zeros_like(tiles)
            return lax.ppermute(tiles, "slab", to_owner)

        return branch

    over = jnp.sum(jnp.where(owner, mask_in, slab_mask)) - FIXED
    which = sum((over > k).astype(jnp.int32) for k in sizes[:-1])
    extra_in = lax.switch(which, [send(k) for k in sizes], extra)

    pair, back = local_call(
        functools.partial(pair_kernel, tile),
        (slab_mask, mask_in, slab_tiles, bulk_in, extra_in, vectors),
        (square, block),
    )
    back_in = lax.ppermute(back, "slab", from_owner)
    first_own, back2 = local_call(first_kernel, (base, pair, vecs_in), (block, block))
    back2, back_in = lax.optimization_barrier((back2, back_in))
    back2_in = lax.ppermute(back2, "slab", from_owner)

    far = local_call(far_kernel, (pair, base_in, back), block)
    own_grp = lax.ppermute(first_own, ("grp", "slab"), role_pairs(True))
    far = local_call(far_kernel, (pair, base_in, back), block)
    first = (base + back_in) / HALF_SPAN
    first_grp = [lax.ppermute(x, ("grp", "slab"), role_pairs(False)) for x in jnp.split(first, 2, axis=0)]
    role = owner.astype(jnp.int32).reshape(1, 1)
    near = local_call(near_kernel, (role, sym, across, first_own, own_grp, first, *first_grp), block)
    total = near + jnp.where(owner, far, back2_in)
    return 2.0 * total / HALF_SPAN - vectors


def solution(mesh):
    spec = P(("grp", "slab"), None)
    return jax.shard_map(body, mesh=mesh, in_specs=(spec,) * 6, out_specs=spec, check_vma=False)
```

```python
import functools

import jax
import jax.numpy as jnp
from jax import lax
from jax.experimental import pallas as pl
from jax.experimental.pallas import tpu as pltpu
from jax.sharding import PartitionSpec as P

CENTER = 0.5
HALF_SPAN = 5.0
FIXED = 12
COST = 1000
GRP_CUTS = 2


def split(x):
    high = x.astype(jnp.bfloat16)
    return high, (x - high.astype(jnp.float32)).astype(jnp.bfloat16)


def product(a, b):
    dot = functools.partial(jnp.dot, preferred_element_type=jnp.float32)
    return dot(a[0], b[0]) + (dot(a[0], b[1]) + dot(a[1], b[0]))


def owns(slab, half):
    return (slab < half) == (slab % 2 == 0)


def pack_kernel(tile, slab_mask, slab_ref, bulk_ref, extra_ref):
    n = slab_ref.shape[0] // tile
    bulk_ref[...] = jnp.zeros_like(bulk_ref)
    extra_ref[...] = jnp.zeros_like(extra_ref)
    tail = (bulk_ref.shape[0] - FIXED * tile, tile)
    row, col = lax.broadcasted_iota(jnp.int32, tail, 0), lax.broadcasted_iota(jnp.int32, tail, 1)
    mask = jnp.zeros(tail, jnp.float32)
    slot = jnp.int32(0)
    for i in range(n):
        for j in range(n):
            at = (slice(i * tile, (i + 1) * tile), slice(j * tile, (j + 1) * tile))
            stored = slab_mask[i, j] > 0
            mask = jnp.where(jnp.logical_and(row == i, col == j), slab_mask[i, j].astype(jnp.float32), mask)

            @pl.when(jnp.logical_and(stored, slot < FIXED))
            def _():
                bulk_ref[pl.ds(pl.multiple_of(slot * tile, tile), tile), :] = slab_ref[at]

            @pl.when(jnp.logical_and(stored, slot >= FIXED))
            def _():
                extra_ref[slot - FIXED] = slab_ref[at]

            slot = slot + stored.astype(jnp.int32)
    bulk_ref[FIXED * tile :, :] = mask


def masked_kernel(tile, mask, tiles_ref, *out_refs):
    n = tiles_ref.shape[0] // tile
    for i in range(n):
        out_ref = out_refs[i * len(out_refs) // n]
        top = i * tile % out_ref.shape[0]
        for j in range(n):
            cols = slice(j * tile, (j + 1) * tile)
            out_ref[top : top + tile, cols] = tiles_ref[i * tile : (i + 1) * tile, cols] * mask[i, j].astype(jnp.float32)


def pair_kernel(tile, own_mask, in_mask, own_ref, bulk_ref, extra_ref, vec_ref, out_ref, back_ref):
    n = own_ref.shape[0] // tile
    for i in range(n):
        for j in range(n):
            at = (slice(i * tile, (i + 1) * tile), slice(j * tile, (j + 1) * tile))
            out_ref[at] = own_ref[at] * own_mask[i, j].astype(jnp.float32)
    slot = jnp.int32(0)
    for i in range(n):
        for j in range(n):
            to = (slice(j * tile, (j + 1) * tile), slice(i * tile, (i + 1) * tile))
            stored = in_mask[i, j] > 0

            @pl.when(jnp.logical_and(stored, slot < FIXED))
            def _():
                out_ref[to] += bulk_ref[pl.ds(pl.multiple_of(slot * tile, tile), tile), :].T

            @pl.when(jnp.logical_and(stored, slot >= FIXED))
            def _():
                out_ref[to] += extra_ref[slot - FIXED].T

            slot = slot + stored.astype(jnp.int32)
    back_ref[...] = product(split(out_ref[...].T), split(vec_ref[...]))


def base_kernel(vec_ref, diag_ref, vec_grp_ref, *refs):
    *grp_refs, low_ref, high_ref, sym_ref, across_ref = refs
    half = len(grp_refs) // 2
    grp, grp_in = (jnp.concatenate([ref[...] for ref in part], axis=0) for part in (grp_refs[:half], grp_refs[half:]))
    raw = diag_ref[...]
    row = lax.broadcasted_iota(jnp.int32, raw.shape, 0)
    col = lax.broadcasted_iota(jnp.int32, raw.shape, 1)
    sym = 0.5 * (raw + raw.T) - jnp.where(row == col, jnp.float32(CENTER), jnp.float32(0))
    across = grp + grp_in.T
    sym_ref[...] = sym
    across_ref[...] = across
    base = product(split(sym), split(vec_ref[...])) + product(split(across), split(vec_grp_ref[...]))
    low_ref[...], high_ref[...] = base[: low_ref.shape[0]], base[low_ref.shape[0] :]


def joined(refs):
    return jnp.concatenate([ref[...] for ref in refs], axis=0)


def first_kernel(low_ref, high_ref, pair_ref, vec_in_ref, first_low_ref, first_high_ref, back_ref):
    pair = pair_ref[...]
    first = (joined((low_ref, high_ref)) + product(split(pair), split(vec_in_ref[...]))) / HALF_SPAN
    first_low_ref[...], first_high_ref[...] = first[: low_ref.shape[0]], first[low_ref.shape[0] :]
    back_ref[...] = product(split(pair.T), split(first))


def near_kernel(sym_ref, across_ref, low_ref, high_ref, grp_low_ref, grp_high_ref, near_ref):
    near_ref[...] = product(split(sym_ref[...]), split(joined((low_ref, high_ref)))) + product(
        split(across_ref[...]), split(joined((grp_low_ref, grp_high_ref)))
    )


def far_kernel(pair_ref, low_ref, high_ref, back_ref, far_ref):
    first = (joined((low_ref, high_ref)) + back_ref[...]) / HALF_SPAN
    far_ref[...] = product(split(pair_ref[...]), split(first))


def local_call(kernel, ins, out_shape):
    spaces = [pl.BlockSpec(memory_space=pltpu.SMEM if x.dtype == jnp.int32 else pltpu.VMEM) for x in ins]
    many = isinstance(out_shape, tuple)
    vmem = pl.BlockSpec(memory_space=pltpu.VMEM)
    return pl.pallas_call(
        kernel,
        out_shape=out_shape,
        in_specs=spaces,
        out_specs=(vmem,) * len(out_shape) if many else vmem,
        compiler_params=pltpu.CompilerParams(vmem_limit_bytes=24 * 1024 * 1024),
        cost_estimate=pl.CostEstimate(flops=COST, bytes_accessed=COST, transcendentals=0),
    )(*ins)


def body(vectors, diag_block, slab_tiles, slab_mask, grp_tiles, grp_mask):
    rows, n_tile = slab_tiles.shape[0], slab_mask.shape[0]
    tile = rows // n_tile
    slots = n_tile * n_tile
    n_slab, n_grp = lax.axis_size("slab"), lax.axis_size("grp")
    half = n_slab // 2
    owner = owns(lax.axis_index("slab"), half)
    to_owner = [(i, i ^ half) for i in range(n_slab) if not owns(i, half)]
    from_owner = [(i, i ^ half) for i in range(n_slab) if owns(i, half)]
    grp_pairs = [(i, i ^ (n_grp // 2)) for i in range(n_grp)]
    f32 = jnp.float32
    square = jax.ShapeDtypeStruct((rows, rows), f32)
    block = jax.ShapeDtypeStruct(vectors.shape, f32)

    vecs_grp = lax.ppermute(vectors, "grp", grp_pairs)
    vecs_in = lax.ppermute(vectors, "slab", to_owner)

    bulk, extra = local_call(
        functools.partial(pack_kernel, tile),
        (slab_mask, slab_tiles),
        (
            jax.ShapeDtypeStruct((FIXED * tile + 8, tile), f32),
            jax.ShapeDtypeStruct((slots - FIXED, tile, tile), f32),
        ),
    )
    bulk_in = lax.ppermute(bulk, "slab", to_owner)
    grp_blocks = local_call(
        functools.partial(masked_kernel, tile),
        (grp_mask, grp_tiles),
        (jax.ShapeDtypeStruct((rows // GRP_CUTS, rows), f32),) * GRP_CUTS,
    )
    grp_in = [lax.ppermute(x, "grp", grp_pairs) for x in grp_blocks]

    half_block = jax.ShapeDtypeStruct((rows // 2, vectors.shape[1]), f32)
    *base, sym, across = local_call(
        base_kernel,
        (vectors, diag_block, vecs_grp, *grp_blocks, *grp_in),
        (half_block, half_block, square, square),
    )
    base_in = [lax.ppermute(x, "slab", to_owner) for x in base]

    base[0], bulk_in = lax.optimization_barrier((base[0], bulk_in))
    mask_in = bulk_in[FIXED * tile : FIXED * tile + n_tile, :n_tile].astype(jnp.int32)
    sizes = (0, slots - FIXED)

    def send(k):
        def branch(tiles):
            if k == 0:
                return jnp.zeros_like(tiles)
            return lax.ppermute(tiles, "slab", to_owner)

        return branch

    over = jnp.sum(jnp.where(owner, mask_in, slab_mask)) - FIXED
    which = sum((over > k).astype(jnp.int32) for k in sizes[:-1])
    extra_in = lax.switch(which, [send(k) for k in sizes], extra)

    pair, back = local_call(
        functools.partial(pair_kernel, tile),
        (slab_mask, mask_in, slab_tiles, bulk_in, extra_in, vectors),
        (square, block),
    )
    back_in = lax.ppermute(back, "slab", from_owner)
    *first_own, back2 = local_call(first_kernel, (*base, pair, vecs_in), (half_block, half_block, block))
    back2, base_in[0] = lax.optimization_barrier((back2, base_in[0]))
    back2_in = lax.ppermute(back2, "slab", from_owner)

    far = local_call(far_kernel, (pair, *base_in, back), block)
    first = [
        jnp.where(owner, own, (part + got) / HALF_SPAN)
        for own, part, got in zip(first_own, base, jnp.split(back_in, 2), strict=True)
    ]
    first_grp = [lax.ppermute(x, "grp", grp_pairs) for x in first]
    near = local_call(near_kernel, (sym, across, *first, *first_grp), block)
    total = near + jnp.where(owner, far, back2_in)
    return 2.0 * total / HALF_SPAN - vectors


def solution(mesh):
    spec = P(("grp", "slab"), None)
    return jax.shard_map(body, mesh=mesh, in_specs=(spec,) * 6, out_specs=spec, check_vma=False)
```

```python
import functools

import jax
import jax.numpy as jnp
from jax import lax
from jax.experimental import pallas as pl
from jax.experimental.pallas import tpu as pltpu
from jax.sharding import PartitionSpec as P

CENTER = 0.5
HALF_SPAN = 5.0
FIXED = 12
COST = 1000
GRP_CUTS = 2


def split(x):
    high = x.astype(jnp.bfloat16)
    return high, (x - high.astype(jnp.float32)).astype(jnp.bfloat16)


def product(a, b):
    dot = functools.partial(jnp.dot, preferred_element_type=jnp.float32)
    return dot(a[0], b[0]) + (dot(a[0], b[1]) + dot(a[1], b[0]))


def owns(slab, half):
    return (slab < half) == (slab % 2 == 0)


def pack_kernel(tile, slab_mask, slab_ref, bulk_ref, extra_ref):
    n = slab_ref.shape[0] // tile
    bulk_ref[...] = jnp.zeros_like(bulk_ref)
    extra_ref[...] = jnp.zeros_like(extra_ref)
    tail = (bulk_ref.shape[0] - FIXED * tile, tile)
    row, col = lax.broadcasted_iota(jnp.int32, tail, 0), lax.broadcasted_iota(jnp.int32, tail, 1)
    mask = jnp.zeros(tail, jnp.float32)
    slot = jnp.int32(0)
    for i in range(n):
        for j in range(n):
            at = (slice(i * tile, (i + 1) * tile), slice(j * tile, (j + 1) * tile))
            stored = slab_mask[i, j] > 0
            mask = jnp.where(jnp.logical_and(row == i, col == j), slab_mask[i, j].astype(jnp.float32), mask)

            @pl.when(jnp.logical_and(stored, slot < FIXED))
            def _():
                bulk_ref[pl.ds(pl.multiple_of(slot * tile, tile), tile), :] = slab_ref[at]

            @pl.when(jnp.logical_and(stored, slot >= FIXED))
            def _():
                extra_ref[slot - FIXED] = slab_ref[at]

            slot = slot + stored.astype(jnp.int32)
    bulk_ref[FIXED * tile :, :] = mask


def masked_kernel(tile, mask, tiles_ref, *out_refs):
    n = tiles_ref.shape[0] // tile
    for i in range(n):
        out_ref = out_refs[i * len(out_refs) // n]
        top = i * tile % out_ref.shape[0]
        for j in range(n):
            cols = slice(j * tile, (j + 1) * tile)
            out_ref[top : top + tile, cols] = tiles_ref[i * tile : (i + 1) * tile, cols] * mask[i, j].astype(jnp.float32)


def pair_kernel(tile, own_mask, in_mask, own_ref, bulk_ref, extra_ref, vec_ref, out_ref, back_ref):
    n = own_ref.shape[0] // tile
    for i in range(n):
        for j in range(n):
            at = (slice(i * tile, (i + 1) * tile), slice(j * tile, (j + 1) * tile))
            out_ref[at] = own_ref[at] * own_mask[i, j].astype(jnp.float32)
    slot = jnp.int32(0)
    for i in range(n):
        for j in range(n):
            to = (slice(j * tile, (j + 1) * tile), slice(i * tile, (i + 1) * tile))
            stored = in_mask[i, j] > 0

            @pl.when(jnp.logical_and(stored, slot < FIXED))
            def _():
                out_ref[to] += bulk_ref[pl.ds(pl.multiple_of(slot * tile, tile), tile), :].T

            @pl.when(jnp.logical_and(stored, slot >= FIXED))
            def _():
                out_ref[to] += extra_ref[slot - FIXED].T

            slot = slot + stored.astype(jnp.int32)
    back_ref[...] = product(split(out_ref[...].T), split(vec_ref[...]))


def base_kernel(vec_ref, diag_ref, vec_grp_ref, *refs):
    *grp_refs, base_ref, sym_ref, across_ref = refs
    half = len(grp_refs) // 2
    grp, grp_in = (jnp.concatenate([ref[...] for ref in part], axis=0) for part in (grp_refs[:half], grp_refs[half:]))
    raw = diag_ref[...]
    row = lax.broadcasted_iota(jnp.int32, raw.shape, 0)
    col = lax.broadcasted_iota(jnp.int32, raw.shape, 1)
    sym = 0.5 * (raw + raw.T) - jnp.where(row == col, jnp.float32(CENTER), jnp.float32(0))
    across = grp + grp_in.T
    sym_ref[...] = sym
    across_ref[...] = across
    base_ref[...] = product(split(sym), split(vec_ref[...])) + product(split(across), split(vec_grp_ref[...]))


def first_kernel(base_ref, pair_ref, vec_in_ref, first_ref, back_ref):
    pair = pair_ref[...]
    first = (base_ref[...] + product(split(pair), split(vec_in_ref[...]))) / HALF_SPAN
    first_ref[...] = first
    back_ref[...] = product(split(pair.T), split(first))


def near_kernel(sym_ref, across_ref, first_ref, *refs):
    *first_grp_refs, near_ref = refs
    first_grp = jnp.concatenate([ref[...] for ref in first_grp_refs], axis=0)
    near_ref[...] = product(split(sym_ref[...]), split(first_ref[...])) + product(
        split(across_ref[...]), split(first_grp)
    )


def far_kernel(pair_ref, base_in_ref, back_ref, far_ref):
    first = (base_in_ref[...] + back_ref[...]) / HALF_SPAN
    far_ref[...] = product(split(pair_ref[...]), split(first))


def local_call(kernel, ins, out_shape):
    spaces = [pl.BlockSpec(memory_space=pltpu.SMEM if x.dtype == jnp.int32 else pltpu.VMEM) for x in ins]
    many = isinstance(out_shape, tuple)
    vmem = pl.BlockSpec(memory_space=pltpu.VMEM)
    return pl.pallas_call(
        kernel,
        out_shape=out_shape,
        in_specs=spaces,
        out_specs=(vmem,) * len(out_shape) if many else vmem,
        compiler_params=pltpu.CompilerParams(vmem_limit_bytes=24 * 1024 * 1024),
        cost_estimate=pl.CostEstimate(flops=COST, bytes_accessed=COST, transcendentals=0),
    )(*ins)


def body(vectors, diag_block, slab_tiles, slab_mask, grp_tiles, grp_mask):
    rows, n_tile = slab_tiles.shape[0], slab_mask.shape[0]
    tile = rows // n_tile
    slots = n_tile * n_tile
    n_slab, n_grp = lax.axis_size("slab"), lax.axis_size("grp")
    half = n_slab // 2
    owner = owns(lax.axis_index("slab"), half)
    to_owner = [(i, i ^ half) for i in range(n_slab) if not owns(i, half)]
    from_owner = [(i, i ^ half) for i in range(n_slab) if owns(i, half)]
    grp_pairs = [(i, i ^ (n_grp // 2)) for i in range(n_grp)]
    f32 = jnp.float32
    square = jax.ShapeDtypeStruct((rows, rows), f32)
    block = jax.ShapeDtypeStruct(vectors.shape, f32)

    vecs_grp = lax.ppermute(vectors, "grp", grp_pairs)
    vecs_in = lax.ppermute(vectors, "slab", to_owner)

    bulk, extra = local_call(
        functools.partial(pack_kernel, tile),
        (slab_mask, slab_tiles),
        (
            jax.ShapeDtypeStruct((FIXED * tile + 8, tile), f32),
            jax.ShapeDtypeStruct((slots - FIXED, tile, tile), f32),
        ),
    )
    bulk_in = lax.ppermute(bulk, "slab", to_owner)
    grp_blocks = local_call(
        functools.partial(masked_kernel, tile),
        (grp_mask, grp_tiles),
        (jax.ShapeDtypeStruct((rows // GRP_CUTS, rows), f32),) * GRP_CUTS,
    )
    grp_in = [lax.ppermute(x, "grp", grp_pairs) for x in grp_blocks]

    base, sym, across = local_call(
        base_kernel, (vectors, diag_block, vecs_grp, *grp_blocks, *grp_in), (block, square, square)
    )
    base, bulk_in = lax.optimization_barrier((base, bulk_in))
    mask_in = bulk_in[FIXED * tile : FIXED * tile + n_tile, :n_tile].astype(jnp.int32)
    sizes = (0, slots - FIXED)

    def send(k):
        def branch(tiles):
            if k == 0:
                return jnp.zeros_like(tiles)
            return lax.ppermute(tiles, "slab", to_owner)

        return branch

    over = jnp.sum(jnp.where(owner, mask_in, slab_mask)) - FIXED
    which = sum((over > k).astype(jnp.int32) for k in sizes[:-1])
    extra_in = lax.switch(which, [send(k) for k in sizes], extra)

    pair, back = local_call(
        functools.partial(pair_kernel, tile),
        (slab_mask, mask_in, slab_tiles, bulk_in, extra_in, vectors),
        (square, block),
    )
    back_in = lax.ppermute(back, "slab", from_owner)
    first_own, back2 = local_call(first_kernel, (base, pair, vecs_in), (block, block))
    back2_in = lax.ppermute(back2, "slab", from_owner)
    later, back_in = lax.optimization_barrier((base, back_in))
    base_in = lax.ppermute(later, "slab", to_owner)

    far = local_call(far_kernel, (pair, base_in, back), block)
    first = jnp.where(owner, first_own, (base + back_in) / HALF_SPAN)
    first_grp = [lax.ppermute(x, "grp", grp_pairs) for x in jnp.split(first, 2, axis=0)]
    near = local_call(near_kernel, (sym, across, first, *first_grp), block)
    total = near + jnp.where(owner, far, back2_in)
    return 2.0 * total / HALF_SPAN - vectors


def solution(mesh):
    spec = P(("grp", "slab"), None)
    return jax.shard_map(body, mesh=mesh, in_specs=(spec,) * 6, out_specs=spec, check_vma=False)
```

```python
import functools

import jax
import jax.numpy as jnp
from jax import lax
from jax.experimental import pallas as pl
from jax.experimental.pallas import tpu as pltpu
from jax.sharding import PartitionSpec as P

CENTER = 0.5
HALF_SPAN = 5.0
FIXED = 12
COST = 1000
GRP_CUTS = 2
CUTS = 2


def split(x):
    high = x.astype(jnp.bfloat16)
    return high, (x - high.astype(jnp.float32)).astype(jnp.bfloat16)


def product(a, b):
    dot = functools.partial(jnp.dot, preferred_element_type=jnp.float32)
    return dot(a[0], b[0]) + (dot(a[0], b[1]) + dot(a[1], b[0]))


def owns(slab, half):
    return (slab < half) == (slab % 2 == 0)


def pack_kernel(tile, slab_mask, slab_ref, bulk_ref, extra_ref):
    n = slab_ref.shape[0] // tile
    bulk_ref[...] = jnp.zeros_like(bulk_ref)
    extra_ref[...] = jnp.zeros_like(extra_ref)
    tail = (bulk_ref.shape[0] - FIXED * tile, tile)
    row, col = lax.broadcasted_iota(jnp.int32, tail, 0), lax.broadcasted_iota(jnp.int32, tail, 1)
    mask = jnp.zeros(tail, jnp.float32)
    slot = jnp.int32(0)
    for i in range(n):
        for j in range(n):
            at = (slice(i * tile, (i + 1) * tile), slice(j * tile, (j + 1) * tile))
            stored = slab_mask[i, j] > 0
            mask = jnp.where(jnp.logical_and(row == i, col == j), slab_mask[i, j].astype(jnp.float32), mask)

            @pl.when(jnp.logical_and(stored, slot < FIXED))
            def _():
                bulk_ref[pl.ds(pl.multiple_of(slot * tile, tile), tile), :] = slab_ref[at]

            @pl.when(jnp.logical_and(stored, slot >= FIXED))
            def _():
                extra_ref[slot - FIXED] = slab_ref[at]

            slot = slot + stored.astype(jnp.int32)
    bulk_ref[FIXED * tile :, :] = mask


def masked_kernel(tile, mask, tiles_ref, *out_refs):
    n = tiles_ref.shape[0] // tile
    for i in range(n):
        out_ref = out_refs[i * len(out_refs) // n]
        top = i * tile % out_ref.shape[0]
        for j in range(n):
            cols = slice(j * tile, (j + 1) * tile)
            out_ref[top : top + tile, cols] = tiles_ref[i * tile : (i + 1) * tile, cols] * mask[i, j].astype(jnp.float32)


def pair_kernel(tile, own_mask, in_mask, own_ref, bulk_ref, extra_ref, vec_ref, out_ref, *back_refs):
    n = own_ref.shape[0] // tile
    for i in range(n):
        for j in range(n):
            at = (slice(i * tile, (i + 1) * tile), slice(j * tile, (j + 1) * tile))
            out_ref[at] = own_ref[at] * own_mask[i, j].astype(jnp.float32)
    slot = jnp.int32(0)
    for i in range(n):
        for j in range(n):
            to = (slice(j * tile, (j + 1) * tile), slice(i * tile, (i + 1) * tile))
            stored = in_mask[i, j] > 0

            @pl.when(jnp.logical_and(stored, slot < FIXED))
            def _():
                out_ref[to] += bulk_ref[pl.ds(pl.multiple_of(slot * tile, tile), tile), :].T

            @pl.when(jnp.logical_and(stored, slot >= FIXED))
            def _():
                out_ref[to] += extra_ref[slot - FIXED].T

            slot = slot + stored.astype(jnp.int32)
    back, top = product(split(out_ref[...].T), split(vec_ref[...])), 0
    for ref in back_refs:
        ref[...] = back[top : top + ref.shape[0]]
        top += ref.shape[0]


def base_kernel(vec_ref, diag_ref, vec_grp_ref, *refs):
    *grp_refs, base_ref, sym_ref, across_ref = refs
    half = len(grp_refs) // 2
    grp, grp_in = (jnp.concatenate([ref[...] for ref in part], axis=0) for part in (grp_refs[:half], grp_refs[half:]))
    raw = diag_ref[...]
    row = lax.broadcasted_iota(jnp.int32, raw.shape, 0)
    col = lax.broadcasted_iota(jnp.int32, raw.shape, 1)
    sym = 0.5 * (raw + raw.T) - jnp.where(row == col, jnp.float32(CENTER), jnp.float32(0))
    across = grp + grp_in.T
    sym_ref[...] = sym
    across_ref[...] = across
    base_ref[...] = product(split(sym), split(vec_ref[...])) + product(split(across), split(vec_grp_ref[...]))


def first_kernel(base_ref, pair_ref, vec_in_ref, first_ref, back_ref):
    pair = pair_ref[...]
    first = (base_ref[...] + product(split(pair), split(vec_in_ref[...]))) / HALF_SPAN
    first_ref[...] = first
    back_ref[...] = product(split(pair.T), split(first))


def step_kernel(top, owner, own_ref, base_ref, back_ref, out_ref):
    rows = slice(top, top + out_ref.shape[0])
    stepped = (base_ref[rows] + back_ref[...]) / HALF_SPAN
    out_ref[...] = jnp.where(owner[0, 0] > 0, own_ref[rows], stepped)


def near_kernel(sym_ref, across_ref, *refs):
    *first_refs, near_ref = refs
    half = len(first_refs) // 2
    first, first_grp = (
        jnp.concatenate([ref[...] for ref in part], axis=0) for part in (first_refs[:half], first_refs[half:])
    )
    near_ref[...] = product(split(sym_ref[...]), split(first)) + product(split(across_ref[...]), split(first_grp))


def far_kernel(pair_ref, base_in_ref, *refs):
    *back_refs, far_ref = refs
    first = (base_in_ref[...] + jnp.concatenate([ref[...] for ref in back_refs], axis=0)) / HALF_SPAN
    far_ref[...] = product(split(pair_ref[...]), split(first))


def local_call(kernel, ins, out_shape):
    spaces = [pl.BlockSpec(memory_space=pltpu.SMEM if x.dtype == jnp.int32 else pltpu.VMEM) for x in ins]
    many = isinstance(out_shape, tuple)
    vmem = pl.BlockSpec(memory_space=pltpu.VMEM)
    return pl.pallas_call(
        kernel,
        out_shape=out_shape,
        in_specs=spaces,
        out_specs=(vmem,) * len(out_shape) if many else vmem,
        compiler_params=pltpu.CompilerParams(vmem_limit_bytes=24 * 1024 * 1024),
        cost_estimate=pl.CostEstimate(flops=COST, bytes_accessed=COST, transcendentals=0),
    )(*ins)


def body(vectors, diag_block, slab_tiles, slab_mask, grp_tiles, grp_mask):
    rows, n_tile = slab_tiles.shape[0], slab_mask.shape[0]
    tile = rows // n_tile
    slots = n_tile * n_tile
    n_slab, n_grp = lax.axis_size("slab"), lax.axis_size("grp")
    half = n_slab // 2
    owner = owns(lax.axis_index("slab"), half)
    to_owner = [(i, i ^ half) for i in range(n_slab) if not owns(i, half)]
    from_owner = [(i, i ^ half) for i in range(n_slab) if owns(i, half)]
    grp_pairs = [(i, i ^ (n_grp // 2)) for i in range(n_grp)]
    f32 = jnp.float32
    square = jax.ShapeDtypeStruct((rows, rows), f32)
    block = jax.ShapeDtypeStruct(vectors.shape, f32)

    vecs_grp = lax.ppermute(vectors, "grp", grp_pairs)
    vecs_in = lax.ppermute(vectors, "slab", to_owner)

    bulk, extra = local_call(
        functools.partial(pack_kernel, tile),
        (slab_mask, slab_tiles),
        (
            jax.ShapeDtypeStruct((FIXED * tile + 8, tile), f32),
            jax.ShapeDtypeStruct((slots - FIXED, tile, tile), f32),
        ),
    )
    bulk_in = lax.ppermute(bulk, "slab", to_owner)
    grp_blocks = local_call(
        functools.partial(masked_kernel, tile),
        (grp_mask, grp_tiles),
        (jax.ShapeDtypeStruct((rows // GRP_CUTS, rows), f32),) * GRP_CUTS,
    )
    grp_in = [lax.ppermute(x, "grp", grp_pairs) for x in grp_blocks]

    base, sym, across = local_call(
        base_kernel, (vectors, diag_block, vecs_grp, *grp_blocks, *grp_in), (block, square, square)
    )
    base, bulk_in = lax.optimization_barrier((base, bulk_in))
    mask_in = bulk_in[FIXED * tile : FIXED * tile + n_tile, :n_tile].astype(jnp.int32)
    sizes = (0, slots - FIXED)

    def send(k):
        def branch(tiles):
            if k == 0:
                return jnp.zeros_like(tiles)
            return lax.ppermute(tiles, "slab", to_owner)

        return branch

    over = jnp.sum(jnp.where(owner, mask_in, slab_mask)) - FIXED
    which = sum((over > k).astype(jnp.int32) for k in sizes[:-1])
    extra_in = lax.switch(which, [send(k) for k in sizes], extra)

    half_block = jax.ShapeDtypeStruct((rows // CUTS, vectors.shape[1]), f32)
    pair, *back = local_call(
        functools.partial(pair_kernel, tile),
        (slab_mask, mask_in, slab_tiles, bulk_in, extra_in, vectors),
        (square,) + (half_block,) * CUTS,
    )
    back_in = [lax.ppermute(x, "slab", from_owner) for x in back]
    first_own, back2 = local_call(first_kernel, (base, pair, vecs_in), (block, block))
    back2_in = lax.ppermute(back2, "slab", from_owner)
    later, back_in[-1] = lax.optimization_barrier((base, back_in[-1]))
    base_in = lax.ppermute(later, "slab", to_owner)

    far = local_call(far_kernel, (pair, base_in, *back), block)
    role = owner.astype(jnp.int32).reshape(1, 1)
    first = [
        local_call(
            functools.partial(step_kernel, at * half_block.shape[0]), (role, first_own, base, got), half_block
        )
        for at, got in enumerate(back_in)
    ]
    first_grp = [lax.ppermute(x, "grp", grp_pairs) for x in first]
    near = local_call(near_kernel, (sym, across, *first, *first_grp), block)
    total = near + jnp.where(owner, far, back2_in)
    return 2.0 * total / HALF_SPAN - vectors


def solution(mesh):
    spec = P(("grp", "slab"), None)
    return jax.shard_map(body, mesh=mesh, in_specs=(spec,) * 6, out_specs=spec, check_vma=False)
```

```python
import functools

import jax
import jax.numpy as jnp
from jax import lax
from jax.experimental import pallas as pl
from jax.experimental.pallas import tpu as pltpu
from jax.sharding import PartitionSpec as P

CENTER = 0.5
HALF_SPAN = 5.0
FIXED = 12
COST = 1000
GRP_CUTS = 2
CUTS = 2


def split(x):
    high = x.astype(jnp.bfloat16)
    return high, (x - high.astype(jnp.float32)).astype(jnp.bfloat16)


def product(a, b):
    dot = functools.partial(jnp.dot, preferred_element_type=jnp.float32)
    return dot(a[0], b[0]) + (dot(a[0], b[1]) + dot(a[1], b[0]))


def owns(slab, half):
    return (slab < half) == (slab % 2 == 0)


def pack_kernel(tile, slab_mask, slab_ref, bulk_ref, extra_ref):
    n = slab_ref.shape[0] // tile
    bulk_ref[...] = jnp.zeros_like(bulk_ref)
    extra_ref[...] = jnp.zeros_like(extra_ref)
    tail = (bulk_ref.shape[0] - FIXED * tile, tile)
    row, col = lax.broadcasted_iota(jnp.int32, tail, 0), lax.broadcasted_iota(jnp.int32, tail, 1)
    mask = jnp.zeros(tail, jnp.float32)
    slot = jnp.int32(0)
    for i in range(n):
        for j in range(n):
            at = (slice(i * tile, (i + 1) * tile), slice(j * tile, (j + 1) * tile))
            stored = slab_mask[i, j] > 0
            mask = jnp.where(jnp.logical_and(row == i, col == j), slab_mask[i, j].astype(jnp.float32), mask)

            @pl.when(jnp.logical_and(stored, slot < FIXED))
            def _():
                bulk_ref[pl.ds(pl.multiple_of(slot * tile, tile), tile), :] = slab_ref[at]

            @pl.when(jnp.logical_and(stored, slot >= FIXED))
            def _():
                extra_ref[slot - FIXED] = slab_ref[at]

            slot = slot + stored.astype(jnp.int32)
    bulk_ref[FIXED * tile :, :] = mask


def masked_kernel(tile, mask, tiles_ref, *out_refs):
    n = tiles_ref.shape[0] // tile
    for i in range(n):
        out_ref = out_refs[i * len(out_refs) // n]
        top = i * tile % out_ref.shape[0]
        for j in range(n):
            cols = slice(j * tile, (j + 1) * tile)
            out_ref[top : top + tile, cols] = tiles_ref[i * tile : (i + 1) * tile, cols] * mask[i, j].astype(jnp.float32)


def pair_kernel(tile, own_mask, in_mask, own_ref, bulk_ref, extra_ref, vec_ref, out_ref, *back_refs):
    n = own_ref.shape[0] // tile
    for i in range(n):
        for j in range(n):
            at = (slice(i * tile, (i + 1) * tile), slice(j * tile, (j + 1) * tile))
            out_ref[at] = own_ref[at] * own_mask[i, j].astype(jnp.float32)
    slot = jnp.int32(0)
    for i in range(n):
        for j in range(n):
            to = (slice(j * tile, (j + 1) * tile), slice(i * tile, (i + 1) * tile))
            stored = in_mask[i, j] > 0

            @pl.when(jnp.logical_and(stored, slot < FIXED))
            def _():
                out_ref[to] += bulk_ref[pl.ds(pl.multiple_of(slot * tile, tile), tile), :].T

            @pl.when(jnp.logical_and(stored, slot >= FIXED))
            def _():
                out_ref[to] += extra_ref[slot - FIXED].T

            slot = slot + stored.astype(jnp.int32)
    back, top = product(split(out_ref[...].T), split(vec_ref[...])), 0
    for ref in back_refs:
        ref[...] = back[top : top + ref.shape[0]]
        top += ref.shape[0]


def base_kernel(vec_ref, diag_ref, vec_grp_ref, *refs):
    *grp_refs, base_ref, sym_ref, across_ref = refs
    half = len(grp_refs) // 2
    grp, grp_in = (jnp.concatenate([ref[...] for ref in part], axis=0) for part in (grp_refs[:half], grp_refs[half:]))
    raw = diag_ref[...]
    row = lax.broadcasted_iota(jnp.int32, raw.shape, 0)
    col = lax.broadcasted_iota(jnp.int32, raw.shape, 1)
    sym = 0.5 * (raw + raw.T) - jnp.where(row == col, jnp.float32(CENTER), jnp.float32(0))
    across = grp + grp_in.T
    sym_ref[...] = sym
    across_ref[...] = across
    base_ref[...] = product(split(sym), split(vec_ref[...])) + product(split(across), split(vec_grp_ref[...]))


def first_kernel(base_ref, pair_ref, vec_in_ref, first_ref, back_ref):
    pair = pair_ref[...]
    first = (base_ref[...] + product(split(pair), split(vec_in_ref[...]))) / HALF_SPAN
    first_ref[...] = first
    back_ref[...] = product(split(pair.T), split(first))


def step_kernel(top, owner, own_ref, base_ref, back_ref, out_ref):
    rows = slice(top, top + out_ref.shape[0])
    stepped = (base_ref[rows] + back_ref[...]) / HALF_SPAN
    out_ref[...] = jnp.where(owner[0, 0] > 0, own_ref[rows], stepped)


def near_kernel(owner, sym_ref, across_ref, back_ref, *refs):
    *first_refs, near_ref = refs
    half = len(first_refs) // 2
    first, first_grp = (
        jnp.concatenate([ref[...] for ref in part], axis=0) for part in (first_refs[:half], first_refs[half:])
    )
    near = product(split(sym_ref[...]), split(first)) + product(split(across_ref[...]), split(first_grp))
    near_ref[...] = near + jnp.where(owner[0, 0] > 0, jnp.float32(0), back_ref[...])


def far_kernel(pair_ref, base_in_ref, *refs):
    *back_refs, far_ref = refs
    first = (base_in_ref[...] + jnp.concatenate([ref[...] for ref in back_refs], axis=0)) / HALF_SPAN
    far_ref[...] = product(split(pair_ref[...]), split(first))


def local_call(kernel, ins, out_shape):
    spaces = [pl.BlockSpec(memory_space=pltpu.SMEM if x.dtype == jnp.int32 else pltpu.VMEM) for x in ins]
    many = isinstance(out_shape, tuple)
    vmem = pl.BlockSpec(memory_space=pltpu.VMEM)
    return pl.pallas_call(
        kernel,
        out_shape=out_shape,
        in_specs=spaces,
        out_specs=(vmem,) * len(out_shape) if many else vmem,
        compiler_params=pltpu.CompilerParams(vmem_limit_bytes=24 * 1024 * 1024),
        cost_estimate=pl.CostEstimate(flops=COST, bytes_accessed=COST, transcendentals=0),
    )(*ins)


def body(vectors, diag_block, slab_tiles, slab_mask, grp_tiles, grp_mask):
    rows, n_tile = slab_tiles.shape[0], slab_mask.shape[0]
    tile = rows // n_tile
    slots = n_tile * n_tile
    n_slab, n_grp = lax.axis_size("slab"), lax.axis_size("grp")
    half = n_slab // 2
    owner = owns(lax.axis_index("slab"), half)
    to_owner = [(i, i ^ half) for i in range(n_slab) if not owns(i, half)]
    from_owner = [(i, i ^ half) for i in range(n_slab) if owns(i, half)]
    grp_pairs = [(i, i ^ (n_grp // 2)) for i in range(n_grp)]
    f32 = jnp.float32
    square = jax.ShapeDtypeStruct((rows, rows), f32)
    block = jax.ShapeDtypeStruct(vectors.shape, f32)

    vecs_grp = lax.ppermute(vectors, "grp", grp_pairs)
    vecs_in = lax.ppermute(vectors, "slab", to_owner)

    bulk, extra = local_call(
        functools.partial(pack_kernel, tile),
        (slab_mask, slab_tiles),
        (
            jax.ShapeDtypeStruct((FIXED * tile + 8, tile), f32),
            jax.ShapeDtypeStruct((slots - FIXED, tile, tile), f32),
        ),
    )
    bulk_in = lax.ppermute(bulk, "slab", to_owner)
    grp_blocks = local_call(
        functools.partial(masked_kernel, tile),
        (grp_mask, grp_tiles),
        (jax.ShapeDtypeStruct((rows // GRP_CUTS, rows), f32),) * GRP_CUTS,
    )
    grp_in = [lax.ppermute(x, "grp", grp_pairs) for x in grp_blocks]

    base, sym, across = local_call(
        base_kernel, (vectors, diag_block, vecs_grp, *grp_blocks, *grp_in), (block, square, square)
    )
    base, bulk_in = lax.optimization_barrier((base, bulk_in))
    mask_in = bulk_in[FIXED * tile : FIXED * tile + n_tile, :n_tile].astype(jnp.int32)
    sizes = (0, slots - FIXED)

    def send(k):
        def branch(tiles):
            if k == 0:
                return jnp.zeros_like(tiles)
            return lax.ppermute(tiles, "slab", to_owner)

        return branch

    over = jnp.sum(jnp.where(owner, mask_in, slab_mask)) - FIXED
    which = sum((over > k).astype(jnp.int32) for k in sizes[:-1])
    extra_in = lax.switch(which, [send(k) for k in sizes], extra)

    half_block = jax.ShapeDtypeStruct((rows // CUTS, vectors.shape[1]), f32)
    pair, *back = local_call(
        functools.partial(pair_kernel, tile),
        (slab_mask, mask_in, slab_tiles, bulk_in, extra_in, vectors),
        (square,) + (half_block,) * CUTS,
    )
    back_in = [lax.ppermute(x, "slab", from_owner) for x in back]
    first_own, back2 = local_call(first_kernel, (base, pair, vecs_in), (block, block))
    back2_in = lax.ppermute(back2, "slab", from_owner)
    later, back_in[-1] = lax.optimization_barrier((base, back_in[-1]))
    base_in = lax.ppermute(later, "slab", to_owner)

    far = local_call(far_kernel, (pair, base_in, *back), block)
    role = owner.astype(jnp.int32).reshape(1, 1)
    first = [
        local_call(
            functools.partial(step_kernel, at * half_block.shape[0]), (role, first_own, base, got), half_block
        )
        for at, got in enumerate(back_in)
    ]
    first_grp = [lax.ppermute(x, "grp", grp_pairs) for x in first]
    near = local_call(near_kernel, (role, sym, across, back2_in, *first, *first_grp), block)
    total = near + jnp.where(owner, far, 0.0)
    return 2.0 * total / HALF_SPAN - vectors


def solution(mesh):
    spec = P(("grp", "slab"), None)
    return jax.shard_map(body, mesh=mesh, in_specs=(spec,) * 6, out_specs=spec, check_vma=False)
```

```python
import functools

import jax
import jax.numpy as jnp
from jax import lax
from jax.experimental import pallas as pl
from jax.experimental.pallas import tpu as pltpu
from jax.sharding import PartitionSpec as P

CENTER = 0.5
HALF_SPAN = 5.0
FIXED = 12
COST = 1000
GRP_CUTS = 2
CUTS = 2


def split(x):
    high = x.astype(jnp.bfloat16)
    return high, (x - high.astype(jnp.float32)).astype(jnp.bfloat16)


def product(a, b):
    dot = functools.partial(jnp.dot, preferred_element_type=jnp.float32)
    return dot(a[0], b[0]) + (dot(a[0], b[1]) + dot(a[1], b[0]))


def owns(slab, half):
    return (slab < half) == (slab % 2 == 0)


def pack_kernel(tile, slab_mask, slab_ref, bulk_ref, extra_ref):
    n = slab_ref.shape[0] // tile
    bulk_ref[...] = jnp.zeros_like(bulk_ref)
    extra_ref[...] = jnp.zeros_like(extra_ref)
    tail = (bulk_ref.shape[0] - FIXED * tile, tile)
    row, col = lax.broadcasted_iota(jnp.int32, tail, 0), lax.broadcasted_iota(jnp.int32, tail, 1)
    mask = jnp.zeros(tail, jnp.float32)
    slot = jnp.int32(0)
    for i in range(n):
        for j in range(n):
            at = (slice(i * tile, (i + 1) * tile), slice(j * tile, (j + 1) * tile))
            stored = slab_mask[i, j] > 0
            mask = jnp.where(jnp.logical_and(row == i, col == j), slab_mask[i, j].astype(jnp.float32), mask)

            @pl.when(jnp.logical_and(stored, slot < FIXED))
            def _():
                bulk_ref[pl.ds(pl.multiple_of(slot * tile, tile), tile), :] = slab_ref[at]

            @pl.when(jnp.logical_and(stored, slot >= FIXED))
            def _():
                extra_ref[slot - FIXED] = slab_ref[at]

            slot = slot + stored.astype(jnp.int32)
    bulk_ref[FIXED * tile :, :] = mask


def masked_kernel(tile, mask, tiles_ref, *out_refs):
    n = tiles_ref.shape[0] // tile
    for i in range(n):
        out_ref = out_refs[i * len(out_refs) // n]
        top = i * tile % out_ref.shape[0]
        for j in range(n):
            cols = slice(j * tile, (j + 1) * tile)
            out_ref[top : top + tile, cols] = tiles_ref[i * tile : (i + 1) * tile, cols] * mask[i, j].astype(jnp.float32)


def pair_kernel(tile, extras, own_mask, in_mask, own_ref, bulk_ref, vec_ref, *refs):
    extra_ref, out_ref, *back_refs = refs if extras else (None, *refs)
    n = own_ref.shape[0] // tile
    for i in range(n):
        for j in range(n):
            at = (slice(i * tile, (i + 1) * tile), slice(j * tile, (j + 1) * tile))
            out_ref[at] = own_ref[at] * own_mask[i, j].astype(jnp.float32)
    slot = jnp.int32(0)
    for i in range(n):
        for j in range(n):
            to = (slice(j * tile, (j + 1) * tile), slice(i * tile, (i + 1) * tile))
            stored = in_mask[i, j] > 0

            @pl.when(jnp.logical_and(stored, slot < FIXED))
            def _():
                out_ref[to] += bulk_ref[pl.ds(pl.multiple_of(slot * tile, tile), tile), :].T

            if extras:

                @pl.when(jnp.logical_and(stored, slot >= FIXED))
                def _():
                    out_ref[to] += extra_ref[slot - FIXED].T

            slot = slot + stored.astype(jnp.int32)
    back, top = product(split(out_ref[...].T), split(vec_ref[...])), 0
    for ref in back_refs:
        ref[...] = back[top : top + ref.shape[0]]
        top += ref.shape[0]


def base_kernel(vec_ref, diag_ref, vec_grp_ref, *refs):
    *grp_refs, base_ref, sym_ref, across_ref = refs
    half = len(grp_refs) // 2
    grp, grp_in = (jnp.concatenate([ref[...] for ref in part], axis=0) for part in (grp_refs[:half], grp_refs[half:]))
    raw = diag_ref[...]
    row = lax.broadcasted_iota(jnp.int32, raw.shape, 0)
    col = lax.broadcasted_iota(jnp.int32, raw.shape, 1)
    sym = 0.5 * (raw + raw.T) - jnp.where(row == col, jnp.float32(CENTER), jnp.float32(0))
    across = grp + grp_in.T
    sym_ref[...] = sym
    across_ref[...] = across
    base_ref[...] = product(split(sym), split(vec_ref[...])) + product(split(across), split(vec_grp_ref[...]))


def first_kernel(base_ref, pair_ref, vec_in_ref, first_ref, back_ref):
    pair = pair_ref[...]
    first = (base_ref[...] + product(split(pair), split(vec_in_ref[...]))) / HALF_SPAN
    first_ref[...] = first
    back_ref[...] = product(split(pair.T), split(first))


def step_kernel(top, owner, own_ref, base_ref, back_ref, out_ref):
    rows = slice(top, top + out_ref.shape[0])
    stepped = (base_ref[rows] + back_ref[...]) / HALF_SPAN
    out_ref[...] = jnp.where(owner[0, 0] > 0, own_ref[rows], stepped)


def near_kernel(owner, sym_ref, across_ref, back_ref, *refs):
    *first_refs, near_ref = refs
    half = len(first_refs) // 2
    first, first_grp = (
        jnp.concatenate([ref[...] for ref in part], axis=0) for part in (first_refs[:half], first_refs[half:])
    )
    near = product(split(sym_ref[...]), split(first)) + product(split(across_ref[...]), split(first_grp))
    near_ref[...] = near + jnp.where(owner[0, 0] > 0, jnp.float32(0), back_ref[...])


def far_kernel(pair_ref, base_in_ref, *refs):
    *back_refs, far_ref = refs
    first = (base_in_ref[...] + jnp.concatenate([ref[...] for ref in back_refs], axis=0)) / HALF_SPAN
    far_ref[...] = product(split(pair_ref[...]), split(first))


def local_call(kernel, ins, out_shape):
    spaces = [pl.BlockSpec(memory_space=pltpu.SMEM if x.dtype == jnp.int32 else pltpu.VMEM) for x in ins]
    many = isinstance(out_shape, tuple)
    vmem = pl.BlockSpec(memory_space=pltpu.VMEM)
    return pl.pallas_call(
        kernel,
        out_shape=out_shape,
        in_specs=spaces,
        out_specs=(vmem,) * len(out_shape) if many else vmem,
        compiler_params=pltpu.CompilerParams(vmem_limit_bytes=24 * 1024 * 1024),
        cost_estimate=pl.CostEstimate(flops=COST, bytes_accessed=COST, transcendentals=0),
    )(*ins)


def body(vectors, diag_block, slab_tiles, slab_mask, grp_tiles, grp_mask):
    rows, n_tile = slab_tiles.shape[0], slab_mask.shape[0]
    tile = rows // n_tile
    slots = n_tile * n_tile
    n_slab, n_grp = lax.axis_size("slab"), lax.axis_size("grp")
    half = n_slab // 2
    owner = owns(lax.axis_index("slab"), half)
    to_owner = [(i, i ^ half) for i in range(n_slab) if not owns(i, half)]
    from_owner = [(i, i ^ half) for i in range(n_slab) if owns(i, half)]
    grp_pairs = [(i, i ^ (n_grp // 2)) for i in range(n_grp)]
    f32 = jnp.float32
    square = jax.ShapeDtypeStruct((rows, rows), f32)
    block = jax.ShapeDtypeStruct(vectors.shape, f32)

    vecs_grp = lax.ppermute(vectors, "grp", grp_pairs)
    vecs_in = lax.ppermute(vectors, "slab", to_owner)

    bulk, extra = local_call(
        functools.partial(pack_kernel, tile),
        (slab_mask, slab_tiles),
        (
            jax.ShapeDtypeStruct((FIXED * tile + 8, tile), f32),
            jax.ShapeDtypeStruct((slots - FIXED, tile, tile), f32),
        ),
    )
    bulk_in = lax.ppermute(bulk, "slab", to_owner)
    grp_blocks = local_call(
        functools.partial(masked_kernel, tile),
        (grp_mask, grp_tiles),
        (jax.ShapeDtypeStruct((rows // GRP_CUTS, rows), f32),) * GRP_CUTS,
    )
    grp_in = [lax.ppermute(x, "grp", grp_pairs) for x in grp_blocks]

    base, sym, across = local_call(
        base_kernel, (vectors, diag_block, vecs_grp, *grp_blocks, *grp_in), (block, square, square)
    )
    base, bulk_in = lax.optimization_barrier((base, bulk_in))
    mask_in = bulk_in[FIXED * tile : FIXED * tile + n_tile, :n_tile].astype(jnp.int32)
    half_block = jax.ShapeDtypeStruct((rows // CUTS, vectors.shape[1]), f32)

    def whole(extras, *ins):
        return local_call(functools.partial(pair_kernel, tile, extras), ins, (square,) + (half_block,) * CUTS)

    def plain(own_mask, in_mask, own, got, vecs, tiles):
        return whole(False, own_mask, in_mask, own, got, vecs)

    def more(own_mask, in_mask, own, got, vecs, tiles):
        return whole(True, own_mask, in_mask, own, got, vecs, lax.ppermute(tiles, "slab", to_owner))

    over = jnp.sum(jnp.where(owner, mask_in, slab_mask)) > FIXED
    pair, *back = lax.cond(over, more, plain, slab_mask, mask_in, slab_tiles, bulk_in, vectors, extra)
    back_in = [lax.ppermute(x, "slab", from_owner) for x in back]
    first_own, back2 = local_call(first_kernel, (base, pair, vecs_in), (block, block))
    back2_in = lax.ppermute(back2, "slab", from_owner)
    later, back_in[-1] = lax.optimization_barrier((base, back_in[-1]))
    base_in = lax.ppermute(later, "slab", to_owner)

    far = local_call(far_kernel, (pair, base_in, *back), block)
    role = owner.astype(jnp.int32).reshape(1, 1)
    first = [
        local_call(
            functools.partial(step_kernel, at * half_block.shape[0]), (role, first_own, base, got), half_block
        )
        for at, got in enumerate(back_in)
    ]
    first_grp = [lax.ppermute(x, "grp", grp_pairs) for x in first]
    near = local_call(near_kernel, (role, sym, across, back2_in, *first, *first_grp), block)
    total = near + jnp.where(owner, far, 0.0)
    return 2.0 * total / HALF_SPAN - vectors


def solution(mesh):
    spec = P(("grp", "slab"), None)
    return jax.shard_map(body, mesh=mesh, in_specs=(spec,) * 6, out_specs=spec, check_vma=False)
```

```python
import functools

import jax
import jax.numpy as jnp
from jax import lax
from jax.experimental import pallas as pl
from jax.experimental.pallas import tpu as pltpu
from jax.sharding import PartitionSpec as P

CENTER = 0.5
HALF_SPAN = 5.0
FIXED = 12
COST = 1000
GRP_CUTS = 2
CUTS = 2


def split(x):
    high = x.astype(jnp.bfloat16)
    return high, (x - high.astype(jnp.float32)).astype(jnp.bfloat16)


def product(a, b):
    dot = functools.partial(jnp.dot, preferred_element_type=jnp.float32)
    return dot(a[0], b[0]) + (dot(a[0], b[1]) + dot(a[1], b[0]))


def owns(slab, half):
    return (slab < half) == (slab % 2 == 0)


def pack_kernel(tile, slab_mask, slab_ref, bulk_ref, extra_ref):
    n = slab_ref.shape[0] // tile
    bulk_ref[...] = jnp.zeros_like(bulk_ref)
    extra_ref[...] = jnp.zeros_like(extra_ref)
    tail = (bulk_ref.shape[0] - FIXED * tile, tile)
    row, col = lax.broadcasted_iota(jnp.int32, tail, 0), lax.broadcasted_iota(jnp.int32, tail, 1)
    mask = jnp.zeros(tail, jnp.float32)
    slot = jnp.int32(0)
    for i in range(n):
        for j in range(n):
            at = (slice(i * tile, (i + 1) * tile), slice(j * tile, (j + 1) * tile))
            stored = slab_mask[i, j] > 0
            mask = jnp.where(jnp.logical_and(row == i, col == j), slab_mask[i, j].astype(jnp.float32), mask)

            @pl.when(jnp.logical_and(stored, slot < FIXED))
            def _():
                bulk_ref[pl.ds(pl.multiple_of(slot * tile, tile), tile), :] = slab_ref[at]

            @pl.when(jnp.logical_and(stored, slot >= FIXED))
            def _():
                extra_ref[slot - FIXED] = slab_ref[at]

            slot = slot + stored.astype(jnp.int32)
    bulk_ref[FIXED * tile :, :] = mask


def masked_kernel(tile, mask, tiles_ref, *out_refs):
    n = tiles_ref.shape[0] // tile
    for i in range(n):
        out_ref = out_refs[i * len(out_refs) // n]
        top = i * tile % out_ref.shape[0]
        for j in range(n):
            cols = slice(j * tile, (j + 1) * tile)
            out_ref[top : top + tile, cols] = tiles_ref[i * tile : (i + 1) * tile, cols] * mask[i, j].astype(jnp.float32)


def pair_kernel(tile, own_mask, in_mask, own_ref, bulk_ref, extra_ref, vec_ref, out_ref, *back_refs):
    n = own_ref.shape[0] // tile
    for i in range(n):
        for j in range(n):
            at = (slice(i * tile, (i + 1) * tile), slice(j * tile, (j + 1) * tile))
            out_ref[at] = own_ref[at] * own_mask[i, j].astype(jnp.float32)
    slot = jnp.int32(0)
    for i in range(n):
        for j in range(n):
            to = (slice(j * tile, (j + 1) * tile), slice(i * tile, (i + 1) * tile))
            stored = in_mask[i, j] > 0

            @pl.when(jnp.logical_and(stored, slot < FIXED))
            def _():
                out_ref[to] += bulk_ref[pl.ds(pl.multiple_of(slot * tile, tile), tile), :].T

            @pl.when(jnp.logical_and(stored, slot >= FIXED))
            def _():
                out_ref[to] += extra_ref[slot - FIXED].T

            slot = slot + stored.astype(jnp.int32)
    back, top = product(split(out_ref[...].T), split(vec_ref[...])), 0
    for ref in back_refs:
        ref[...] = back[top : top + ref.shape[0]]
        top += ref.shape[0]


def base_kernel(vec_ref, diag_ref, vec_grp_ref, *refs):
    *grp_refs, base_ref, sym_ref, across_ref = refs
    half = len(grp_refs) // 2
    grp, grp_in = (jnp.concatenate([ref[...] for ref in part], axis=0) for part in (grp_refs[:half], grp_refs[half:]))
    raw = diag_ref[...]
    row = lax.broadcasted_iota(jnp.int32, raw.shape, 0)
    col = lax.broadcasted_iota(jnp.int32, raw.shape, 1)
    sym = 0.5 * (raw + raw.T) - jnp.where(row == col, jnp.float32(CENTER), jnp.float32(0))
    across = grp + grp_in.T
    sym_ref[...] = sym
    across_ref[...] = across
    base_ref[...] = product(split(sym), split(vec_ref[...])) + product(split(across), split(vec_grp_ref[...]))


def first_kernel(base_ref, pair_ref, vec_in_ref, first_ref, back_ref):
    pair = pair_ref[...]
    first = (base_ref[...] + product(split(pair), split(vec_in_ref[...]))) / HALF_SPAN
    first_ref[...] = first
    back_ref[...] = product(split(pair.T), split(first))


def step_kernel(top, owner, own_ref, base_ref, back_ref, out_ref):
    rows = slice(top, top + out_ref.shape[0])
    stepped = (base_ref[rows] + back_ref[...]) / HALF_SPAN
    out_ref[...] = jnp.where(owner[0, 0] > 0, own_ref[rows], stepped)


def near_kernel(owner, sym_ref, across_ref, back_ref, *refs):
    *first_refs, near_ref = refs
    half = len(first_refs) // 2
    first, first_grp = (
        jnp.concatenate([ref[...] for ref in part], axis=0) for part in (first_refs[:half], first_refs[half:])
    )
    near = product(split(sym_ref[...]), split(first)) + product(split(across_ref[...]), split(first_grp))
    near_ref[...] = near + jnp.where(owner[0, 0] > 0, jnp.float32(0), back_ref[...])


def far_kernel(pair_ref, base_in_ref, *refs):
    *back_refs, far_ref = refs
    first = (base_in_ref[...] + jnp.concatenate([ref[...] for ref in back_refs], axis=0)) / HALF_SPAN
    far_ref[...] = product(split(pair_ref[...]), split(first))


def local_call(kernel, ins, out_shape):
    spaces = [pl.BlockSpec(memory_space=pltpu.SMEM if x.dtype == jnp.int32 else pltpu.VMEM) for x in ins]
    many = isinstance(out_shape, tuple)
    vmem = pl.BlockSpec(memory_space=pltpu.VMEM)
    return pl.pallas_call(
        kernel,
        out_shape=out_shape,
        in_specs=spaces,
        out_specs=(vmem,) * len(out_shape) if many else vmem,
        compiler_params=pltpu.CompilerParams(vmem_limit_bytes=24 * 1024 * 1024),
        cost_estimate=pl.CostEstimate(flops=COST, bytes_accessed=COST, transcendentals=0),
    )(*ins)


def body(vectors, diag_block, slab_tiles, slab_mask, grp_tiles, grp_mask):
    rows, n_tile = slab_tiles.shape[0], slab_mask.shape[0]
    tile = rows // n_tile
    slots = n_tile * n_tile
    n_slab, n_grp = lax.axis_size("slab"), lax.axis_size("grp")
    half = n_slab // 2
    owner = owns(lax.axis_index("slab"), half)
    to_owner = [(i, i ^ half) for i in range(n_slab) if not owns(i, half)]
    from_owner = [(i, i ^ half) for i in range(n_slab) if owns(i, half)]
    grp_pairs = [(i, i ^ (n_grp // 2)) for i in range(n_grp)]
    f32 = jnp.float32
    square = jax.ShapeDtypeStruct((rows, rows), f32)
    block = jax.ShapeDtypeStruct(vectors.shape, f32)

    vecs_grp = lax.ppermute(vectors, "grp", grp_pairs)
    vecs_in = lax.ppermute(vectors, "slab", to_owner)

    bulk, extra = local_call(
        functools.partial(pack_kernel, tile),
        (slab_mask, slab_tiles),
        (
            jax.ShapeDtypeStruct((FIXED * tile + 8, tile), f32),
            jax.ShapeDtypeStruct((slots - FIXED, tile, tile), f32),
        ),
    )
    bulk_in = lax.ppermute(bulk, "slab", to_owner)
    grp_blocks = local_call(
        functools.partial(masked_kernel, tile),
        (grp_mask, grp_tiles),
        (jax.ShapeDtypeStruct((rows // GRP_CUTS, rows), f32),) * GRP_CUTS,
    )
    grp_in = [lax.ppermute(x, "grp", grp_pairs) for x in grp_blocks]

    base, sym, across = local_call(
        base_kernel, (vectors, diag_block, vecs_grp, *grp_blocks, *grp_in), (block, square, square)
    )
    base, bulk_in = lax.optimization_barrier((base, bulk_in))
    mask_in = bulk_in[FIXED * tile : FIXED * tile + n_tile, :n_tile].astype(jnp.int32)
    sizes = (0, slots - FIXED)

    def send(k):
        def branch(tiles):
            if k == 0:
                return jnp.zeros_like(tiles)
            return lax.ppermute(tiles, "slab", to_owner)

        return branch

    over = jnp.sum(jnp.where(owner, mask_in, slab_mask)) - FIXED
    which = sum((over > k).astype(jnp.int32) for k in sizes[:-1])
    extra_in = lax.switch(which, [send(k) for k in sizes], extra)

    half_block = jax.ShapeDtypeStruct((rows // CUTS, vectors.shape[1]), f32)
    pair, *back = local_call(
        functools.partial(pair_kernel, tile),
        (slab_mask, mask_in, slab_tiles, bulk_in, extra_in, vectors),
        (square,) + (half_block,) * CUTS,
    )
    back_in = [lax.ppermute(x, "slab", from_owner) for x in back]
    first_own, back2 = local_call(first_kernel, (base, pair, vecs_in), (block, block))
    back2_in = lax.ppermute(back2, "slab", from_owner)
    later, *_ = lax.optimization_barrier((base, *back_in))
    base_in = lax.ppermute(later, "slab", to_owner)

    far = local_call(far_kernel, (pair, base_in, *back), block)
    role = owner.astype(jnp.int32).reshape(1, 1)
    first = [
        local_call(
            functools.partial(step_kernel, at * half_block.shape[0]), (role, first_own, base, got), half_block
        )
        for at, got in enumerate(back_in)
    ]
    first_grp = [lax.ppermute(x, "grp", grp_pairs) for x in first]
    near = local_call(near_kernel, (role, sym, across, back2_in, *first, *first_grp), block)
    total = near + jnp.where(owner, far, 0.0)
    return 2.0 * total / HALF_SPAN - vectors


def solution(mesh):
    spec = P(("grp", "slab"), None)
    return jax.shard_map(body, mesh=mesh, in_specs=(spec,) * 6, out_specs=spec, check_vma=False)
```
